256 devices in a mesh: section: 8 (over z), dp: 32 (over y, x, core).
Axes of the slice: x: 4, y: 4, z: 8, core: 2. Of those that a mesh axis runs over, the one named last changes fastest.
Arguments:
- inputs: bfloat16 [4096, 4608], P('dp'), may hold values from -6 to 6
- w_in: bfloat16 [8, 4608, 128], P('section'), may hold values from -0.09375 to 0.09375
- w_out: bfloat16 [8, 128, 4608], P('section'), may hold values from -0.5 to 0.5
- layer_scale: float32 [8, 4608], P('section'), may hold values from 0.1 to 1.6, as said below
- cotangent: bfloat16 [4096, 4608], P('dp'), may hold values from -200 to 200
Outputs:
- grad_in: float32 [8, 4608, 128], P('section', 'dp')
- grad_out: float32 [8, 128, 4608], P('section', 'dp')
The draws below stay inside these ranges and needn't reach their ends.
Inputs may be any that keep to these rules, and one draw needn't show every extreme that they name: `layer_scale`: positive scales.
All inputs are finite; a program needn't handle non-finite values.
Results may differ from the reference program's by a relative error of at most 0.028.
Values may be sent and summed in bfloat16 or wider, within the bound.
No kernel may reach another device: no remote copies, remote signals or barrier semaphores. Data moves between devices by JAX's collectives and lax.ppermute only.
A program may use at most 64 MiB of HBM per device.

```python
import math
import jax
import jax.numpy as jnp
from jax import lax

D = 4608
R = 128
SEQ = 128
SECTIONS = 8
TOKENS = 4096


def draw_layer_scale(key, part):
    key = jax.random.fold_in(key, 11)
    ladder = jnp.arange(SECTIONS, dtype=jnp.float32)[:, None] / (SECTIONS - 1)
    channel = jnp.exp(jax.random.uniform(key, (SECTIONS, D), jnp.float32, math.log(0.25), 0.0))
    return channel * (0.6 + 0.6 * ladder)


def draw_cotangent(key, part):
    key = jax.random.fold_in(key, 23)
    subkeys = jax.random.split(key, 3)
    col_scale = jnp.exp(jax.random.uniform(subkeys[2], (1, D), jnp.float32, 0.0, math.log(4.0)))
    entries = jnp.clip(jax.random.normal(subkeys[0], (TOKENS, D), jnp.float32), -5.0, 5.0)
    row_scale = jnp.exp(jax.random.uniform(subkeys[1], (TOKENS, 1), jnp.float32, 0.0, math.log(10.0)))
    return (entries * row_scale * col_scale).astype(jnp.bfloat16)


def raised(values, key, source, target, blocks, factor):
    def block_of(position):
        return (jnp.arange(values.shape[position]) // (values.shape[position] // blocks)).reshape((-1,) + (1,) * (values.ndim - 1 - position))

    one_side = jax.random.permutation(key, blocks)[block_of(target)]
    second = (block_of(target) + blocks // 2) % blocks
    return jnp.where((block_of(source) == one_side) | (block_of(source) == second), factor * values, values)


def block_scale(key, dims, shards, low, high):
    factor_of = 1.0
    for dim, shards_of in shards:
        draws = jax.random.uniform(jax.random.fold_in(jax.random.fold_in(key, 6), dim), (shards_of,), jnp.float32, low / len(shards), high / len(shards))
        factor_of = factor_of * jnp.repeat(jnp.exp(draws), dims[dim] // shards_of).reshape((-1,) + (1,) * (len(dims) - 1 - dim))
    return factor_of


def gaussian(rng, extent, deviation, reach, shards=(), held_as=jnp.bfloat16):
    factor_of = block_scale(rng, extent, shards, -0.22, 0.18) if shards else 1.0
    values = jax.random.normal(rng, extent, jnp.float32) * deviation * factor_of
    return jnp.minimum(jnp.maximum(values, -reach), reach).astype(held_as)


def noise_with(stream_key, dims, width, most, pieces, heavy, kind=jnp.bfloat16):
    values = width * jax.random.normal(stream_key, dims, jnp.float32)
    if pieces:
        values = values * block_scale(stream_key, dims, pieces, -0.22, 0.18)
    return jnp.clip(raised(values, jax.random.fold_in(stream_key, 3), *heavy), -most, most).astype(kind)


def setup_inputs(seed: int = 0) -> dict:
    splits = jax.random.split(jax.random.key(seed), 6)
    inputs = noise_with(splits[0], (TOKENS, D), 1.0, 6.0, ((0, 32),), (0, 1, 32, 2.75))
    w_in = gaussian(splits[1], (SECTIONS, D, R), D ** -0.5, 0.09375, ((0, 8),))
    w_out = gaussian(splits[2], (SECTIONS, R, D), R ** -0.5, 0.5, ((0, 8),))
    layer_scale = draw_layer_scale(jax.random.fold_in(splits[5], 71), 0)
    cotangent = draw_cotangent(jax.random.fold_in(splits[5], 71), 0)
    return dict(inputs=inputs, w_in=w_in, w_out=w_out, layer_scale=layer_scale, cotangent=cotangent)


EPS = 1e-06
CLIP_NORM = 256.0
CLIP_OFFSET = 0.01

def row_scale(current):
    widened = current.astype(jnp.float32)
    inv_rms = lax.rsqrt(lax.optimization_barrier(jnp.mean(widened * widened, axis=1, keepdims=True)) + EPS)
    return (widened, inv_rms)

def gram_norms(first_op, second_op):
    left_rows = first_op.astype(jnp.float32).reshape(-1, SEQ, first_op.shape[1])
    right_rows = second_op.astype(jnp.float32).reshape(-1, SEQ, second_op.shape[1])
    left_gram = jnp.einsum('eia,eja->eij', left_rows, left_rows)
    right_gram = jnp.einsum('eia,eja->eij', right_rows, right_rows)
    return lax.optimization_barrier(jnp.sum(left_gram * right_gram, axis=(1, 2)))

def reference(inputs, w_in, w_out, layer_scale, cotangent):
    section_count = w_in.shape[0]
    examples = inputs.shape[0] // SEQ
    current = inputs
    stored = []
    for section_index in range(section_count):
        widened, inv_rms = row_scale(current)
        normed = (widened * inv_rms).astype(jnp.bfloat16)
        pre_act = jnp.dot(normed, w_in[section_index], preferred_element_type=jnp.float32)
        hidden = jax.nn.gelu(pre_act).astype(jnp.bfloat16)
        branch = jnp.dot(hidden, w_out[section_index], preferred_element_type=jnp.float32)
        stored.append((current, normed, pre_act, hidden))
        current = (widened + layer_scale[section_index].astype(jnp.float32) * branch).astype(jnp.bfloat16)
    incoming = cotangent
    sq_norms = jnp.zeros((examples,), jnp.float32)
    kept = [None] * section_count
    for section_index in reversed(range(section_count)):
        current, normed, pre_act, hidden = stored[section_index]
        wide_grad = incoming.astype(jnp.float32)
        out_grad = (layer_scale[section_index].astype(jnp.float32) * wide_grad).astype(jnp.bfloat16)
        hidden_grad = jnp.dot(out_grad, w_out[section_index].T, preferred_element_type=jnp.float32)
        _, pullback = jax.vjp(jax.nn.gelu, pre_act)
        pre_grad = pullback(hidden_grad)[0].astype(jnp.bfloat16)
        sq_norms = sq_norms + gram_norms(hidden, out_grad) + gram_norms(normed, pre_grad)
        kept[section_index] = (out_grad, pre_grad)
        if section_index > 0:
            normed_grad = jnp.dot(pre_grad, w_in[section_index].T, preferred_element_type=jnp.float32)
            widened, inv_rms = row_scale(current)
            unit_rows = widened * inv_rms
            center = lax.optimization_barrier(jnp.mean(normed_grad * unit_rows, axis=1, keepdims=True))
            incoming = (wide_grad + inv_rms * (normed_grad - unit_rows * center)).astype(jnp.bfloat16)
    clip_factor = CLIP_NORM / (jnp.sqrt(sq_norms) + CLIP_OFFSET)
    row_factor = jnp.repeat(clip_factor, SEQ)[:, None]
    grads_in = []
    grads_out = []
    for section_index in range(section_count):
        current, normed, pre_act, hidden = stored[section_index]
        out_grad, pre_grad = kept[section_index]
        scaled_out = (out_grad.astype(jnp.float32) * row_factor).astype(jnp.bfloat16)
        scaled_in = (pre_grad.astype(jnp.float32) * row_factor).astype(jnp.bfloat16)
        grads_out.append(jnp.dot(hidden.T, scaled_out, preferred_element_type=jnp.float32))
        grads_in.append(jnp.dot(normed.T, scaled_in, preferred_element_type=jnp.float32))
    return (jnp.stack(grads_in), jnp.stack(grads_out))
```

```python
import jax
import jax.numpy as jnp
import numpy as np
from jax import lax
from jax.experimental import pallas as pl
from jax.experimental.pallas import tpu as pltpu
from jax.sharding import Mesh, PartitionSpec as P

EPS = 1e-06
CLIP_NORM = 256.0
CLIP_OFFSET = 0.01
S = 8
R = 128
T = 128
D = 4608
SLICE = D // S
QUARTER = SLICE // 4
Z, Y, X, C = "section", "y", "x", "core"
BF = jnp.bfloat16
F32 = jnp.float32
NN = (((1,), (0,)), ((), ()))
NT = (((1,), (1,)), ((), ()))
GELU_A = 0.7978845608028654
GELU_B = 0.044715
VMEM_LIMIT = 48 * 1024 * 1024


def mm(a, b, dims=NN):
    return lax.dot_general(a, b, dims, preferred_element_type=F32)


def halves(even, odd):
    low = lax.broadcasted_iota(jnp.int32, even.shape, 1) < 4
    return (
        jnp.where(low, even, pltpu.roll(odd, 4, axis=1)),
        jnp.where(low, pltpu.roll(even, 4, axis=1), odd),
    )


def chain_kernel(core_ref, own_ref, oth_ref, proj_ref, sq_ref, h_ref, ht_ref, p_ref, scal_ref, kmat, pre, qacc, hacc, slope):
    first = core_ref[0] == 0

    def place(s, carry):
        cols = pl.ds(pl.multiple_of(s * R, R), R)
        for x in range(4):
            own = [own_ref[s, y, x].astype(F32).reshape(4, 8, R) for y in range(4)]
            oth = [oth_ref[s, y, x].astype(F32).reshape(4, 8, R) for y in range(4)]
            for c in range(2):
                v = [jnp.where(first, a, b) if c == 0 else jnp.where(first, b, a) for a, b in zip(own, oth)]
                e01, o01 = halves(v[0], v[1])
                e23, o23 = halves(v[2], v[3])
                ev = jnp.concatenate([e01, e23], axis=1).astype(BF)
                od = jnp.concatenate([o01, o23], axis=1).astype(BF)
                for i in range(4):
                    row = (x * 2 + c) * 16
                    kmat[2 * i * R + row : 2 * i * R + row + 16, cols] = ev[i]
                    kmat[(2 * i + 1) * R + row : (2 * i + 1) * R + row + 16, cols] = od[i]
        return carry

    lax.fori_loop(0, S, place, 0)
    for s in range(S):
        block = proj_ref[s].astype(F32)
        pre[:, s * R : (s + 1) * R] = block[:, :R]
        qacc[:, s * R : (s + 1) * R] = block[:, R : 2 * R]
        hacc[:, s * R : (s + 1) * R] = block[:, 2 * R :]
    sq = sq_ref[...]
    lane = lax.broadcasted_iota(jnp.int32, (T, R), 1)
    scal = jnp.zeros((T, R), F32)
    inv = []
    for s in range(S):
        here = slice(s * R, (s + 1) * R)
        r = lax.rsqrt(sq * (1.0 / D) + EPS)
        inv.append(r)
        scal = jnp.where(lane == s, r, scal)
        v = pre[:, here] * r
        pre[:, here] = v
        th = jnp.tanh(GELU_A * (v + GELU_B * v * v * v))
        h = (0.5 * v * (1.0 + th)).astype(BF)
        slope[:, here] = 0.5 * (1.0 + th) + 0.5 * v * (1.0 - th * th) * (GELU_A * (1.0 + 3.0 * GELU_B * v * v))
        h_ref[s] = h
        hf = h.astype(F32)
        ht_ref[s] = hf.T.astype(BF)
        if s + 1 < S:
            before = qacc[:, here]
            qacc[:, s * R :] += mm(h, kmat[s * R :, here], NT)
            sq = sq + jnp.sum(hf * (before + qacc[:, here]), axis=1, keepdims=True)
            pre[:, (s + 1) * R :] += mm(h, kmat[here, (s + 1) * R :])
    gam = jnp.zeros((T, 1), F32)
    for s in reversed(range(S)):
        here = slice(s * R, (s + 1) * R)
        hg = hacc[:, here]
        if s + 1 < S:
            hg = hg - gam * qacc[:, here]
        p = (hg * slope[:, here]).astype(BF)
        p_ref[s] = p
        r = inv[s]
        cen = r * r * (jnp.sum(p.astype(F32) * pre[:, here], axis=1, keepdims=True) * (1.0 / D))
        scal = jnp.where(lane == S + s, cen, scal)
        if s > 0:
            upd = r * mm(p, kmat[: s * R, here], NT)
            if s + 1 < S:
                upd = upd - gam * mm(h_ref[s], kmat[here, : s * R])
            hacc[:, : s * R] += upd
        gam = gam + cen
    scal_ref[...] = scal.T[: 2 * S]


def chain(core, own, oth, proj, sq):
    vm = pl.BlockSpec(memory_space=pltpu.VMEM)
    return pl.pallas_call(
        chain_kernel,
        out_shape=(
            jax.ShapeDtypeStruct((S, T, R), BF),
            jax.ShapeDtypeStruct((S, R, T), BF),
            jax.ShapeDtypeStruct((S, T, R), BF),
            jax.ShapeDtypeStruct((2 * S, T), F32),
        ),
        in_specs=[pl.BlockSpec(memory_space=pltpu.SMEM), vm, vm, vm, vm],
        out_specs=(vm, vm, vm, vm),
        scratch_shapes=[
            pltpu.VMEM((S * R, S * R), BF),
            pltpu.VMEM((T, S * R), F32),
            pltpu.VMEM((T, S * R), F32),
            pltpu.VMEM((T, S * R), F32),
            pltpu.VMEM((T, S * R), F32),
        ],
        compiler_params=pltpu.CompilerParams(vmem_limit_bytes=VMEM_LIMIT),
        cost_estimate=pl.CostEstimate(flops=2 * 192 * T * R * R, bytes_accessed=6 << 20, transcendentals=S * T * R),
        name="chain",
    )(core, own, oth, proj, sq)


def grads_kernel(core_ref, wown_ref, woth_ref, xt_ref, ct_ref, ls_ref, h_ref, ht_ref, p_ref, scal_ref, gi_ref, go_ref, sq_ref, xs, gos):
    core = core_ref[0]
    first = core == 0
    total = jnp.zeros((SLICE // 4, R), F32)

    def pick(flip, s):
        a, b = wown_ref[:, s], woth_ref[:, s]
        return (jnp.where(first, b, a) if flip else jnp.where(first, a, b)).reshape(SLICE, R)

    x = xt_ref[...]
    for s in range(S):
        xs[s] = x
        xf = x.astype(F32)
        n = (xf * scal_ref[s : s + 1, :]).astype(BF)
        gi = mm(n, p_ref[s])
        for j in range(4):
            part = gi[j * QUARTER : (j + 1) * QUARTER]
            total = total + part * part
            gi_ref[core ^ (j % 2), s * 2 + j // 2] = part.astype(BF)
        if s + 1 < S:
            x = (xf + mm(pick(True, s), h_ref[s], NT)).astype(BF)
    g = ct_ref[...]
    for s in reversed(range(S)):
        gos[s] = mm(ht_ref[s], g, NT) * ls_ref[s]
        if s > 0:
            m = mm(pick(False, s), p_ref[s], NT)
            g = (g.astype(F32) + scal_ref[s : s + 1, :] * m - scal_ref[S + s : S + s + 1, :] * xs[s].astype(F32)).astype(BF)
    acc = jnp.zeros((R, SLICE), F32)
    for s in range(S):
        acc = acc + gos[s] * gos[s]
    for quad in range(2):
        v = [gos[quad * 4 + i].reshape(16, 8, SLICE) for i in range(4)]
        a0, a1 = halves(v[0], v[1])
        b0, b1 = halves(v[2], v[3])
        go_ref[core, :, quad * 16 : (quad + 1) * 16] = jnp.concatenate([a0, b0], axis=1).astype(BF)
        go_ref[core ^ 1, :, quad * 16 : (quad + 1) * 16] = jnp.concatenate([a1, b1], axis=1).astype(BF)
    one = jnp.sum(jnp.sum(total, axis=0, keepdims=True), axis=1, keepdims=True)
    two = jnp.sum(jnp.sum(acc, axis=0, keepdims=True), axis=1, keepdims=True)
    sq_ref[...] = jnp.broadcast_to(one + two, (8, 128))


def grads(core, wown, woth, xt, ct, ls, h, ht, p, scal):
    vm = pl.BlockSpec(memory_space=pltpu.VMEM)
    return pl.pallas_call(
        grads_kernel,
        out_shape=(
            jax.ShapeDtypeStruct((2, 16, QUARTER, R), BF),
            jax.ShapeDtypeStruct((2, 16, 32, SLICE), BF),
            jax.ShapeDtypeStruct((8, 128), F32),
        ),
        in_specs=[pl.BlockSpec(memory_space=pltpu.SMEM)] + [vm] * 9,
        out_specs=(vm, vm, vm),
        scratch_shapes=[pltpu.VMEM((S, SLICE, T), BF), pltpu.VMEM((S, R, SLICE), F32)],
        compiler_params=pltpu.CompilerParams(vmem_limit_bytes=VMEM_LIMIT),
        cost_estimate=pl.CostEstimate(flops=2 * 32 * SLICE * T * R, bytes_accessed=6 << 20, transcendentals=0),
        name="grads",
    )(core, wown, woth, xt, ct, ls, h, ht, p, scal)


def per_device(inputs, w_in, w_out, layer_scale, cotangent):
    w1 = w_in[0]
    scale = layer_scale[0]
    z, y, x, c = (lax.axis_index(a) for a in (Z, Y, X, C))
    core = c.reshape(1).astype(jnp.int32)
    w2 = (w_out[0].astype(F32) * scale).astype(BF)

    q = (x * 2 + c) * 4 + y
    mine = lax.dynamic_slice_in_dim(w2, q * 4, 4, 0)
    rows = lax.all_to_all(jnp.broadcast_to(mine, (S, 4, D)), Z, 0, 0).reshape(S * 4, D)

    v1 = lax.dynamic_index_in_dim(w1.reshape(S, 4, QUARTER, R), x, 1, keepdims=False)
    v2 = lax.dynamic_index_in_dim(w2.reshape(R, S, 4, QUARTER), x, 2, keepdims=False)
    v2 = jnp.transpose(v2, (1, 2, 0))
    piece = lax.all_to_all(jnp.where(c == 0, v1, v2), Z, 0, 0)
    wown = lax.all_gather(piece, X, axis=0)
    woth = lax.ppermute(wown, C, [(0, 1), (1, 0)])
    ls = lax.all_to_all(scale.reshape(S, 1, SLICE), Z, 0, 0)

    proj = jnp.concatenate([mm(inputs, w1), mm(inputs, w2, NT), mm(cotangent, w2, NT)], axis=1).astype(BF)
    proj = lax.all_to_all(jnp.broadcast_to(proj, (S, T, 3 * R)), Z, 0, 0)
    wide = inputs.astype(F32)
    sq = jnp.sum(wide * wide, axis=1, keepdims=True)
    xt = lax.dynamic_slice_in_dim(inputs, z * SLICE, SLICE, 1).T
    ct = lax.dynamic_slice_in_dim(cotangent, z * SLICE, SLICE, 1).T

    below = (lax.broadcasted_iota(jnp.int32, (S * 4, R), 0) // 4) < z
    kpart = jnp.where(below, mm(rows, w1), mm(rows, w2, NT)).astype(BF)
    kown = lax.all_to_all(jnp.broadcast_to(kpart, (S * 16, S * 4, R)), (Z, Y, X), 0, 0)
    koth = lax.ppermute(kown, C, [(0, 1), (1, 0)])
    h, ht, p, scal = chain(
        core, kown.reshape(S, 4, 4, S * 4, R), koth.reshape(S, 4, 4, S * 4, R), proj, sq
    )

    gi, go, part = grads(core, wown, woth, xt, ct, ls, h, ht, p, scal)
    swap = [(0, 1), (1, 0)]
    total = lax.psum(part[:1, :1], Z)
    factor = CLIP_NORM / (jnp.sqrt(total) + CLIP_OFFSET)
    other = lax.ppermute(factor, C, swap)
    gi_got = lax.ppermute(gi[1], C, swap)
    go_got = lax.ppermute(go[1], C, swap)
    gi_sum = (gi[0].astype(F32) * factor + gi_got.astype(F32) * other).astype(BF)
    go_sum = (go[0].astype(F32) * factor + go_got.astype(F32) * other).astype(BF)

    gi_all = lax.all_to_all(gi_sum, (Y, X), 0, 0)
    go_all = lax.all_to_all(go_sum, (Y, X), 0, 0)
    gi_row = jnp.sum(gi_all.astype(F32), axis=0).astype(BF)
    route = [(k * 32 + s * 4 + j, s * 32 + k * 4 + j) for k in range(S) for s in range(S) for j in range(4)]
    grad_in = lax.ppermute(gi_row, (Z, Y, X, C), route).astype(F32)
    go_row = jnp.sum(go_all.astype(F32), axis=0).astype(BF).reshape(S, 4, SLICE)
    grad_out = lax.all_to_all(go_row, Z, 0, 0).astype(F32)
    grad_out = jnp.transpose(grad_out, (1, 0, 2)).reshape(4, D)
    return grad_in[None], grad_out[None]


def solution(mesh):
    split = Mesh(np.asarray(mesh.devices).reshape(S, 4, 4, 2), (Z, Y, X, C))
    dp = (Y, X, C)
    return jax.shard_map(
        per_device,
        mesh=split,
        in_specs=(P(dp, None), P(Z, None, None), P(Z, None, None), P(Z, None), P(dp, None)),
        out_specs=(P(Z, dp, None), P(Z, dp, None)),
        check_vma=False,
    )
```

```python
import jax
import jax.numpy as jnp
import numpy as np
from jax import lax
from jax.experimental import pallas as pl
from jax.experimental.pallas import tpu as pltpu
from jax.sharding import Mesh, PartitionSpec as P

EPS = 1e-06
CLIP_NORM = 256.0
CLIP_OFFSET = 0.01
S = 8
R = 128
T = 128
D = 4608
SLICE = D // S
QUARTER = SLICE // 4
Z, Y, X, C = "section", "y", "x", "core"
BF = jnp.bfloat16
F32 = jnp.float32
NN = (((1,), (0,)), ((), ()))
NT = (((1,), (1,)), ((), ()))
GELU_A = 0.7978845608028654
GELU_B = 0.044715
VMEM_LIMIT = 48 * 1024 * 1024
HALF = D // 2
ROWS = D * 4 // R
VM = pl.BlockSpec(memory_space=pltpu.VMEM)
SM = pl.BlockSpec(memory_space=pltpu.SMEM)


def mm(a, b, dims=NN):
    return lax.dot_general(a, b, dims, preferred_element_type=F32)


def halves(even, odd):
    low = lax.broadcasted_iota(jnp.int32, even.shape, 1) < 4
    return (
        jnp.where(low, even, pltpu.roll(odd, 4, axis=1)),
        jnp.where(low, pltpu.roll(even, 4, axis=1), odd),
    )


def call(kernel, name, outs, ins, scratch=(), flops=0, size=1 << 21, trans=0):
    return pl.pallas_call(
        kernel,
        out_shape=tuple(jax.ShapeDtypeStruct(*o) for o in outs),
        in_specs=list(ins),
        out_specs=(VM,) * len(outs),
        scratch_shapes=list(scratch),
        compiler_params=pltpu.CompilerParams(vmem_limit_bytes=VMEM_LIMIT),
        cost_estimate=pl.CostEstimate(flops=flops, bytes_accessed=size, transcendentals=trans),
        name=name,
    )


def pack_kernel(at_ref, w_in_ref, w_out_ref, ls_ref, w2_ref, pay_ref, turned):
    x, core, q = at_ref[1], at_ref[2], at_ref[3]
    ls = ls_ref[...]
    w2 = (w_out_ref[...].astype(F32) * ls).astype(BF)
    w2_ref[...] = w2
    row = lax.broadcasted_iota(jnp.int32, (8, R), 0) % 4
    col = lax.broadcasted_iota(jnp.int32, (8, R), 1)
    mine = mm((col == q * 4 + row).astype(BF), w2)
    low = lax.broadcasted_iota(jnp.int32, (8, HALF), 0) < 4
    mine = jnp.where(low, mine[:, :HALF], mine[:, HALF:])
    for u in range(9):
        two = jnp.concatenate([mine[:, 256 * u : 256 * u + R], mine[:, 256 * u + R : 256 * (u + 1)]], axis=0).astype(BF)
        for k in range(S):
            pay_ref[k, 16 * u : 16 * u + 16] = two
    top = ls.astype(BF).astype(F32)
    low_part = ls - top
    for k in range(S):
        rows = []
        for part in (top, low_part):
            rows += [part[:, SLICE * k + R * j : SLICE * k + R * (j + 1)] for j in range(4)]
            tail = part[:, SLICE * k + 512 : SLICE * (k + 1)]
            rows.append(jnp.concatenate([tail, tail], axis=1))
        rows.append(jnp.zeros((6, R), F32))
        pay_ref[k, 2 * ROWS : 2 * ROWS + 16] = jnp.concatenate(rows, axis=0).astype(BF)

    @pl.when(core == 0)
    def _():
        for k in range(S):
            start = pl.multiple_of(SLICE * k + QUARTER * x, 16)
            pay_ref[k, ROWS : 2 * ROWS] = w_in_ref[pl.ds(start, QUARTER), :]

    @pl.when(core != 0)
    def _():
        for t in range(D // R):
            turned[t * R : (t + 1) * R, :] = w2_ref[:, t * R : (t + 1) * R].astype(F32).T.astype(BF)
        for k in range(S):
            start = pl.multiple_of(SLICE * k + QUARTER * x, 16)
            pay_ref[k, ROWS : 2 * ROWS] = turned[pl.ds(start, QUARTER), :]


def project_kernel(at_ref, x_ref, c_ref, w_in_ref, w2_ref, proj_ref, sq_ref, xt_ref, ct_ref, wide):
    z = at_ref[0]
    xv = x_ref[...]
    w2 = w2_ref[...]
    proj_ref[:, :R] = mm(xv, w_in_ref[...]).astype(BF)
    proj_ref[:, R : 2 * R] = mm(xv, w2, NT).astype(BF)
    proj_ref[:, 2 * R : 3 * R] = mm(c_ref[...], w2, NT).astype(BF)
    proj_ref[:, 3 * R :] = jnp.zeros((T, R), BF)
    xf = xv.astype(F32)
    sq_ref[...] = jnp.sum(xf * xf, axis=1, keepdims=True)
    base = pl.multiple_of(((z * 9) // 2) * R, R)
    off = pl.multiple_of((z % 2) * 64, 16)
    for src, dst in ((x_ref, xt_ref), (c_ref, ct_ref)):
        for t in range(5):
            wide[t * R : (t + 1) * R, :] = src[:, pl.ds(base + t * R, R)].astype(F32).T.astype(BF)
        dst[...] = wide[pl.ds(off, SLICE), :]


def gram_kernel(at_ref, got_ref, w_in_ref, w2_ref, out_ref):
    z = at_ref[0]
    first, second = [], []
    for u in range(9):
        block = got_ref[:, 16 * u : 16 * u + 16, :].astype(F32)
        for part in (block[:, :8], block[:, 8:]):
            part = part.reshape(4, 2, 8, R)
            a, b = halves(part[:, 0], part[:, 1])
            first.append(a.reshape(32, R).astype(BF))
            second.append(b.reshape(32, R).astype(BF))
    first = jnp.concatenate(first, axis=1)
    second = jnp.concatenate(second, axis=1)
    up = mm(first, w_in_ref[:HALF]) + mm(second, w_in_ref[HALF:])
    down = mm(first, w2_ref[:, :HALF], NT) + mm(second, w2_ref[:, HALF:], NT)
    below = (lax.broadcasted_iota(jnp.int32, (32, R), 0) // 4) < z
    out = jnp.where(below, up, down).astype(BF)
    for k in range(S):
        out_ref[k] = out


def main_kernel(at_ref, own_ref, oth_ref, proj_ref, sq_ref, wown_ref, woth_ref, xt_ref, ct_ref, ls_ref, gown_ref, goth_ref, norm_ref, kmat, pre, qacc, hacc, slope, hs, hts, ps, sts, wbuf, xs, gos, sem):
    xpos, core = at_ref[1], at_ref[2]
    is0 = core == 0
    copies = []
    for i in range(4):
        slot = (xpos + 4 - i) % 4
        for n, (ref, half) in enumerate(((wown_ref, core), (woth_ref, 1 - core))):
            copies.append(pltpu.make_async_copy(ref.at[i], wbuf.at[half, slot], sem.at[i * 2 + n]))
    for cp in copies:
        cp.start()

    def place(s, carry):
        cols = pl.ds(pl.multiple_of(s * R, R), R)
        for x in range(4):
            own = [own_ref[y * 4 + x, s].astype(F32).reshape(4, 8, R) for y in range(4)]
            oth = [oth_ref[y * 4 + x, s].astype(F32).reshape(4, 8, R) for y in range(4)]
            for c in range(2):
                v = [jnp.where(is0, a, b) if c == 0 else jnp.where(is0, b, a) for a, b in zip(own, oth)]
                e01, o01 = halves(v[0], v[1])
                e23, o23 = halves(v[2], v[3])
                ev = jnp.concatenate([e01, e23], axis=1).astype(BF)
                od = jnp.concatenate([o01, o23], axis=1).astype(BF)
                for i in range(4):
                    row = (x * 2 + c) * 16
                    kmat[2 * i * R + row : 2 * i * R + row + 16, cols] = ev[i]
                    kmat[(2 * i + 1) * R + row : (2 * i + 1) * R + row + 16, cols] = od[i]
        return carry

    lax.fori_loop(0, S, place, 0)
    for s in range(S):
        block = proj_ref[s].astype(F32)
        pre[:, s * R : (s + 1) * R] = block[:, :R]
        qacc[:, s * R : (s + 1) * R] = block[:, R : 2 * R]
        hacc[:, s * R : (s + 1) * R] = block[:, 2 * R : 3 * R]
    sq = sq_ref[...]
    lane = lax.broadcasted_iota(jnp.int32, (T, R), 1)
    scal = jnp.zeros((T, R), F32)
    inv = []
    for s in range(S):
        here = slice(s * R, (s + 1) * R)
        r = lax.rsqrt(sq * (1.0 / D) + EPS)
        inv.append(r)
        scal = jnp.where(lane == s, r, scal)
        v = pre[:, here] * r
        pre[:, here] = v
        th = jnp.tanh(GELU_A * (v + GELU_B * v * v * v))
        h = (0.5 * v * (1.0 + th)).astype(BF)
        slope[:, here] = 0.5 * (1.0 + th) + 0.5 * v * (1.0 - th * th) * (GELU_A * (1.0 + 3.0 * GELU_B * v * v))
        hs[s] = h
        hf = h.astype(F32)
        hts[s] = hf.T.astype(BF)
        if s + 1 < S:
            before = qacc[:, here]
            qacc[:, s * R :] += mm(h, kmat[s * R :, here], NT)
            sq = sq + jnp.sum(hf * (before + qacc[:, here]), axis=1, keepdims=True)
            pre[:, (s + 1) * R :] += mm(h, kmat[here, (s + 1) * R :])
    gam = jnp.zeros((T, 1), F32)
    for s in reversed(range(S)):
        here = slice(s * R, (s + 1) * R)
        hg = hacc[:, here]
        if s + 1 < S:
            hg = hg - gam * qacc[:, here]
        p = (hg * slope[:, here]).astype(BF)
        ps[s] = p
        r = inv[s]
        cen = r * r * (jnp.sum(p.astype(F32) * pre[:, here], axis=1, keepdims=True) * (1.0 / D))
        scal = jnp.where(lane == S + s, cen, scal)
        if s > 0:
            upd = r * mm(p, kmat[: s * R, here], NT)
            if s + 1 < S:
                upd = upd - gam * mm(hs[s], kmat[here, : s * R])
            hacc[:, : s * R] += upd
        gam = gam + cen
    sts[...] = scal.T
    for cp in copies:
        cp.wait()

    total = jnp.zeros((QUARTER, R), F32)
    x = xt_ref[...]
    for s in range(S):
        xs[s] = x
        xf = x.astype(F32)
        n = (xf * sts[s : s + 1, :]).astype(BF)
        gi = mm(n, ps[s])
        for j1 in range(2):
            a = gi[2 * j1 * QUARTER : (2 * j1 + 1) * QUARTER]
            b = gi[(2 * j1 + 1) * QUARTER : (2 * j1 + 2) * QUARTER]
            total = total + a * a + b * b
            gown_ref[s * 2 + j1, :ROWS] = jnp.where(is0, a, b).astype(BF)
            goth_ref[s * 2 + j1, :ROWS] = jnp.where(is0, b, a).astype(BF)
        if s + 1 < S:
            x = (xf + mm(wbuf[1, :, s].reshape(SLICE, R), hs[s], NT)).astype(BF)
    g = ct_ref[...]
    for s in reversed(range(S)):
        lsf = ls_ref[s].astype(F32)
        lsf = lsf[:5] + lsf[5:10]
        lrow = jnp.concatenate([lsf[j : j + 1] for j in range(4)] + [lsf[4:5, :64]], axis=1)
        gos[s] = mm(hts[s], g, NT) * lrow
        if s > 0:
            m = mm(wbuf[0, :, s].reshape(SLICE, R), ps[s], NT)
            g = (g.astype(F32) + sts[s : s + 1, :] * m - sts[S + s : S + s + 1, :] * xs[s].astype(F32)).astype(BF)
    acc = jnp.zeros((R, SLICE), F32)
    for s in range(S):
        acc = acc + gos[s] * gos[s]
    tails = []
    for quad in range(2):
        v = [gos[quad * 4 + i].reshape(16, 8, SLICE) for i in range(4)]
        a0, a1 = halves(v[0], v[1])
        b0, b1 = halves(v[2], v[3])
        even = jnp.concatenate([a0, b0], axis=1)
        odd = jnp.concatenate([a1, b1], axis=1)
        mine = jnp.where(is0, even, odd)
        rest = jnp.where(is0, odd, even)
        for t in range(4):
            at = slice(ROWS + 32 * t + 16 * quad, ROWS + 32 * t + 16 * quad + 16)
            gown_ref[:, at] = mine[:, :, t * R : (t + 1) * R].astype(BF)
            goth_ref[:, at] = rest[:, :, t * R : (t + 1) * R].astype(BF)
        tails.append((mine[:, :, 4 * R :], rest[:, :, 4 * R :]))
    gown_ref[:, ROWS + 128 :] = jnp.concatenate([tails[0][0], tails[1][0]], axis=2).astype(BF)
    goth_ref[:, ROWS + 128 :] = jnp.concatenate([tails[0][1], tails[1][1]], axis=2).astype(BF)
    one = jnp.sum(jnp.sum(total, axis=0, keepdims=True), axis=1, keepdims=True)
    two = jnp.sum(jnp.sum(acc, axis=0, keepdims=True), axis=1, keepdims=True)
    norm_ref[...] = jnp.broadcast_to((one + two).reshape(1, 1, 1), (S, 8, R))


def sum_kernel(got_ref, gi_ref, go_ref):
    total = got_ref[0].astype(F32)
    for i in range(1, 16):
        total = total + got_ref[i].astype(F32)
    gi_ref[...] = total[:ROWS].astype(BF)
    go = total[ROWS:]
    last = go[4 * 32 :]
    tail = jnp.concatenate([last[:, :64], last[:, 64:]], axis=0)
    go = jnp.concatenate([go[32 * t : 32 * t + 32] for t in range(4)] + [tail], axis=1).reshape(4, 8, SLICE)
    for i in range(4):
        go_ref[2 * i] = go[i]
        go_ref[2 * i + 1] = pltpu.roll(go[i], 4, axis=0)


def join_kernel(got_ref, out_ref):
    out_ref[0] = jnp.concatenate([got_ref[k, :4] for k in range(S)], axis=1)


def per_device(inputs, w_in, w_out, layer_scale, cotangent):
    z, y, x, c = (lax.axis_index(a) for a in (Z, Y, X, C))
    at = jnp.stack([z, x, c, (x * 2 + c) * 4 + y]).astype(jnp.int32)
    swap = [(0, 1), (1, 0)]
    w1 = w_in[0]
    flops = 2 * T * D * R

    w2, pay = call(
        pack_kernel, "pack",
        [((R, D), BF), ((S, 2 * ROWS + 16, R), BF)],
        [SM, VM, VM, VM],
        [pltpu.VMEM((D, R), BF)], flops=flops // 16, size=4 << 20,
    )(at, w1, w_out[0], layer_scale)
    got = lax.all_to_all(pay, Z, 0, 0)

    proj, sq, xt, ct = call(
        project_kernel, "project",
        [((T, 4 * R), BF), ((T, 1), F32), ((SLICE, T), BF), ((SLICE, T), BF)],
        [SM, VM, VM, VM, VM],
        [pltpu.VMEM((5 * R, T), BF)], flops=3 * flops, size=5 << 20,
    )(at, inputs, cotangent, w1, w2)
    proj = lax.all_gather(proj, Z, axis=0)

    (part,) = call(gram_kernel, "gram", [((S, 32, R), BF)], [SM, VM, VM, VM], flops=flops // 2, size=3 << 20)(at, got, w1, w2)
    part = lax.all_to_all(part, Z, 0, 0)
    piece = got[:, ROWS : 2 * ROWS]
    shifts = [lax.ppermute(piece, X, [(i, (i + d) % 4) for i in range(4)]) for d in (1, 2, 3)]
    wown = jnp.stack([piece] + shifts)
    woth = lax.ppermute(wown, C, swap)
    ls = got[:, 2 * ROWS :]

    kown = lax.all_to_all(jnp.broadcast_to(part, (16, S, 32, R)), (Y, X), 0, 0)
    koth = lax.ppermute(kown, C, swap)

    anywhere = pl.BlockSpec(memory_space=pl.ANY)
    gown, goth, norm = call(
        main_kernel, "main",
        [((16, 2 * ROWS, R), BF), ((16, 2 * ROWS, R), BF), ((S, 8, R), F32)],
        [SM, VM, VM, VM, VM, anywhere, anywhere, VM, VM, VM],
        [
            pltpu.VMEM((S * R, S * R), BF),
            pltpu.VMEM((T, S * R), F32),
            pltpu.VMEM((T, S * R), F32),
            pltpu.VMEM((T, S * R), F32),
            pltpu.VMEM((T, S * R), F32),
            pltpu.VMEM((S, T, R), BF),
            pltpu.VMEM((S, R, T), BF),
            pltpu.VMEM((S, T, R), BF),
            pltpu.VMEM((R, T), F32),
            pltpu.VMEM((2, 4, S, QUARTER, R), BF),
            pltpu.VMEM((S, SLICE, T), BF),
            pltpu.VMEM((S, R, SLICE), F32),
            pltpu.SemaphoreType.DMA((8,)),
        ],
        flops=2 * 32 * SLICE * T * R + 2 * 192 * T * R * R, size=10 << 20, trans=S * T * R,
    )(at, kown, koth, proj, sq, wown, woth, xt, ct, ls)

    ggot = lax.ppermute(goth, C, swap)
    total = jnp.sum(lax.all_to_all(norm, Z, 0, 0), axis=0)
    factor = CLIP_NORM / (jnp.sqrt(total) + CLIP_OFFSET)
    other = lax.ppermute(factor, C, swap)
    both = (gown.astype(F32) * factor[0, 0] + ggot.astype(F32) * other[0, 0]).astype(BF)
    both = lax.all_to_all(both, (Y, X), 0, 0)
    gi, go = call(sum_kernel, "sum", [((ROWS, R), BF), ((S, 8, SLICE), F32)], [VM], size=2 << 20)(both)
    route = [(k * 32 + s * 4 + j, s * 32 + k * 4 + j) for k in range(S) for s in range(S) for j in range(4)]
    grad_in = lax.ppermute(gi, (Z, Y, X, C), route).astype(F32)[None]
    go = lax.all_to_all(go, Z, 0, 0)
    (grad_out,) = call(join_kernel, "join", [((1, 4, D), F32)], [VM])(go)
    return grad_in, grad_out


def solution(mesh):
    split = Mesh(np.asarray(mesh.devices).reshape(S, 4, 4, 2), (Z, Y, X, C))
    dp = (Y, X, C)
    return jax.shard_map(
        per_device,
        mesh=split,
        in_specs=(P(dp, None), P(Z, None, None), P(Z, None, None), P(Z, None), P(dp, None)),
        out_specs=(P(Z, dp, None), P(Z, dp, None)),
        check_vma=False,
    )
```

```python
import jax
import jax.numpy as jnp
import numpy as np
from jax import lax
from jax.experimental import pallas as pl
from jax.experimental.pallas import tpu as pltpu
from jax.sharding import Mesh, PartitionSpec as P

EPS = 1e-06
CLIP_NORM = 256.0
CLIP_OFFSET = 0.01
S = 8
R = 128
T = 128
D = 4608
SLICE = D // S
QUARTER = SLICE // 4
PACK_VMEM = 60
Z, Y, X, C = "section", "y", "x", "core"
BF = jnp.bfloat16
F32 = jnp.float32
NN = (((1,), (0,)), ((), ()))
NT = (((1,), (1,)), ((), ()))
GELU_A = 0.7978845608028654
GELU_B = 0.044715
HALF = D // 2
ROWS = D * 4 // R
VM = pl.BlockSpec(memory_space=pltpu.VMEM)


def mm(a, b, dims=NN):
    return lax.dot_general(a, b, dims, preferred_element_type=F32)


def halves(even, odd):
    low = lax.broadcasted_iota(jnp.int32, even.shape, 1) < 4
    return (
        jnp.where(low, even, pltpu.roll(odd, 4, axis=1)),
        jnp.where(low, pltpu.roll(even, 4, axis=1), odd),
    )


def call(kernel, name, outs, ins, scratch=(), flops=0, size=1 << 21, trans=0, vmem=8):
    return pl.pallas_call(
        kernel,
        out_shape=tuple(jax.ShapeDtypeStruct(*o) for o in outs),
        in_specs=list(ins),
        out_specs=(VM,) * len(outs),
        scratch_shapes=list(scratch),
        compiler_params=pltpu.CompilerParams(vmem_limit_bytes=vmem << 20),
        cost_estimate=pl.CostEstimate(flops=flops, bytes_accessed=size, transcendentals=trans),
        name=name,
    )


def pack_kernel(w_in_ref, w_out_ref, ls_ref, w2_ref, pay_ref, wide, turned, sem):
    y, x, core = lax.axis_index(Y), lax.axis_index(X), lax.axis_index(C)
    q = (x * 2 + core) * 4 + y
    step = D // 4
    loads = [
        pltpu.make_async_copy(w_out_ref.at[:, pl.ds(i * step, step)], wide.at[:, pl.ds(i * step, step)], sem.at[i])
        for i in range(4)
    ]
    for cp in loads:
        cp.start()

    def piece(k):
        return pl.ds(pl.multiple_of(SLICE * k + QUARTER * x, 16), QUARTER)

    def feature_copies():
        return [
            pltpu.make_async_copy(w_in_ref.at[piece(k)], pay_ref.at[k, pl.ds(ROWS, QUARTER)], sem.at[4 + k])
            for k in range(S)
        ]

    @pl.when(core == 0)
    def _():
        for cp in feature_copies():
            cp.start()

    ls = ls_ref[...]
    top = ls.astype(BF).astype(F32)
    low_part = ls - top
    for k in range(S):
        rows = []
        for part in (top, low_part):
            rows += [part[:, SLICE * k + R * j : SLICE * k + R * (j + 1)] for j in range(4)]
            tail = part[:, SLICE * k + 512 : SLICE * (k + 1)]
            rows.append(jnp.concatenate([tail, tail], axis=1))
        rows.append(jnp.zeros((6, R), F32))
        pay_ref[k, 2 * ROWS : 2 * ROWS + 16] = jnp.concatenate(rows, axis=0).astype(BF)
    row = lax.broadcasted_iota(jnp.int32, (8, R), 0) % 4
    col = lax.broadcasted_iota(jnp.int32, (8, R), 1)
    pick = (col == q * 4 + row).astype(BF)
    mine = []
    for i, cp in enumerate(loads):
        cp.wait()
        at = slice(i * step, (i + 1) * step)
        part = (wide[:, at].astype(F32) * ls[:, at]).astype(BF)
        w2_ref[:, at] = part
        mine.append(mm(pick, part))
    mine = jnp.concatenate(mine, axis=1)
    low = lax.broadcasted_iota(jnp.int32, (8, HALF), 0) < 4
    mine = jnp.where(low, mine[:, :HALF], mine[:, HALF:])
    for u in range(9):
        two = jnp.concatenate([mine[:, 256 * u : 256 * u + R], mine[:, 256 * u + R : 256 * (u + 1)]], axis=0).astype(BF)
        for k in range(S):
            pay_ref[k, 16 * u : 16 * u + 16] = two

    @pl.when(core == 0)
    def _():
        for cp in feature_copies():
            cp.wait()

    @pl.when(core != 0)
    def _():
        for t in range(D // R):
            turned[t * R : (t + 1) * R, :] = w2_ref[:, t * R : (t + 1) * R].astype(F32).T.astype(BF)
        for k in range(S):
            pay_ref[k, ROWS : 2 * ROWS] = turned[piece(k), :]


def project_kernel(x_ref, c_ref, w_in_ref, w2_ref, proj_ref, sq_ref, xt_ref, ct_ref, wide):
    z = lax.axis_index(Z)
    xv = x_ref[...]
    w2 = w2_ref[...]
    proj_ref[:, :R] = mm(xv, w_in_ref[...]).astype(BF)
    proj_ref[:, R : 2 * R] = mm(xv, w2, NT).astype(BF)
    proj_ref[:, 2 * R :] = mm(c_ref[...], w2, NT).astype(BF)
    xf = xv.astype(F32)
    sq_ref[...] = jnp.sum(xf * xf, axis=1, keepdims=True)
    base = pl.multiple_of(((z * 9) // 2) * R, R)
    off = pl.multiple_of((z % 2) * 64, 16)
    for src, dst in ((x_ref, xt_ref), (c_ref, ct_ref)):
        for t in range(5):
            wide[t * R : (t + 1) * R, :] = src[:, pl.ds(base + t * R, R)].astype(F32).T.astype(BF)
        dst[...] = wide[pl.ds(off, SLICE), :]


def gram_kernel(got_ref, w_in_ref, w2_ref, proj_ref, out_ref):
    z = lax.axis_index(Z)
    first, second = [], []
    for u in range(9):
        block = got_ref[:, 16 * u : 16 * u + 16, :].astype(F32)
        for part in (block[:, :8], block[:, 8:]):
            part = part.reshape(4, 2, 8, R)
            a, b = halves(part[:, 0], part[:, 1])
            first.append(a.reshape(32, R).astype(BF))
            second.append(b.reshape(32, R).astype(BF))
    first = jnp.concatenate(first, axis=1)
    second = jnp.concatenate(second, axis=1)
    up = mm(first, w_in_ref[:HALF]) + mm(second, w_in_ref[HALF:])
    down = mm(first, w2_ref[:, :HALF], NT) + mm(second, w2_ref[:, HALF:], NT)
    below = (lax.broadcasted_iota(jnp.int32, (32, R), 0) // 4) < z
    out = jnp.where(below, up, down).astype(BF)
    for k in range(S):
        out_ref[k, :32] = out
        for i in range(3):
            out_ref[k, 32 + T * i : 32 + T * (i + 1)] = proj_ref[:, i * R : (i + 1) * R]


def main_kernel(own_ref, oth_ref, *refs):
    proj_ref, sq_ref, wown_ref, woth_ref, xt_ref, ct_ref, ls_ref, gown_ref, goth_ref, norm_ref = refs[:10]
    kmat, pre, qacc, hacc, slope, hs, hts, ps, sts, wbuf, xs, gos, sem = refs[10:]
    core = lax.axis_index(C)
    is0 = core == 0
    copies = []
    for i in range(4):
        slot = (lax.axis_index(X) + 4 - i) % 4
        for n, (ref, half) in enumerate(((wown_ref, core), (woth_ref, 1 - core))):
            copies.append(pltpu.make_async_copy(ref.at[i], wbuf.at[half, slot], sem.at[i * 2 + n]))
    for cp in copies:
        cp.start()

    def place(s, carry):
        cols = pl.ds(pl.multiple_of(s * R, R), R)
        for x in range(4):
            own = [own_ref[y * 4 + x, s].astype(F32).reshape(4, 8, R) for y in range(4)]
            oth = [oth_ref[y * 4 + x, s].astype(F32).reshape(4, 8, R) for y in range(4)]
            for c in range(2):
                v = [jnp.where(is0, a, b) if c == 0 else jnp.where(is0, b, a) for a, b in zip(own, oth)]
                e01, o01 = halves(v[0], v[1])
                e23, o23 = halves(v[2], v[3])
                ev = jnp.concatenate([e01, e23], axis=1).astype(BF)
                od = jnp.concatenate([o01, o23], axis=1).astype(BF)
                for i in range(4):
                    row = (x * 2 + c) * 16
                    kmat[2 * i * R + row : 2 * i * R + row + 16, cols] = ev[i]
                    kmat[(2 * i + 1) * R + row : (2 * i + 1) * R + row + 16, cols] = od[i]
        return carry

    lax.fori_loop(0, S, place, 0)
    for s in range(S):
        for i, acc in enumerate((pre, qacc, hacc)):
            acc[:, s * R : (s + 1) * R] = proj_ref[s, 32 + T * i : 32 + T * (i + 1)].astype(F32)
    sq = sq_ref[...]
    lane = lax.broadcasted_iota(jnp.int32, (T, R), 1)
    scal = jnp.zeros((T, R), F32)
    inv = []
    for s in range(S):
        here = slice(s * R, (s + 1) * R)
        r = lax.rsqrt(sq * (1.0 / D) + EPS)
        inv.append(r)
        scal = jnp.where(lane == s, r, scal)
        v = pre[:, here] * r
        pre[:, here] = v
        th = jnp.tanh(GELU_A * (v + GELU_B * v * v * v))
        h = (0.5 * v * (1.0 + th)).astype(BF)
        slope[:, here] = 0.5 * (1.0 + th) + 0.5 * v * (1.0 - th * th) * (GELU_A * (1.0 + 3.0 * GELU_B * v * v))
        hs[s] = h
        hf = h.astype(F32)
        hts[s] = hf.T.astype(BF)
        if s + 1 < S:
            before = qacc[:, here]
            qacc[:, s * R :] += mm(h, kmat[s * R :, here], NT)
            sq = sq + jnp.sum(hf * (before + qacc[:, here]), axis=1, keepdims=True)
            pre[:, (s + 1) * R :] += mm(h, kmat[here, (s + 1) * R :])
    gam = jnp.zeros((T, 1), F32)
    for s in reversed(range(S)):
        here = slice(s * R, (s + 1) * R)
        hg = hacc[:, here]
        if s + 1 < S:
            hg = hg - gam * qacc[:, here]
        p = (hg * slope[:, here]).astype(BF)
        ps[s] = p
        r = inv[s]
        cen = r * r * (jnp.sum(p.astype(F32) * pre[:, here], axis=1, keepdims=True) * (1.0 / D))
        scal = jnp.where(lane == S + s, cen, scal)
        if s > 0:
            upd = r * mm(p, kmat[: s * R, here], NT)
            if s + 1 < S:
                upd = upd - gam * mm(hs[s], kmat[here, : s * R])
            hacc[:, : s * R] += upd
        gam = gam + cen
    sts[...] = scal.T
    for cp in copies:
        cp.wait()

    def weights(kind, s):
        return wbuf[kind, :, s].reshape(SLICE, R)

    total = jnp.zeros((QUARTER, R), F32)
    x = xt_ref[...]
    for s in range(S):
        xs[s] = x
        xf = x.astype(F32)
        n = (xf * sts[s : s + 1, :]).astype(BF)
        gi = mm(n, ps[s])
        for j1 in range(2):
            a = gi[2 * j1 * QUARTER : (2 * j1 + 1) * QUARTER]
            b = gi[(2 * j1 + 1) * QUARTER : (2 * j1 + 2) * QUARTER]
            total = total + a * a + b * b
            gown_ref[s * 2 + j1, :ROWS] = jnp.where(is0, a, b).astype(BF)
            goth_ref[s * 2 + j1, :ROWS] = jnp.where(is0, b, a).astype(BF)
        if s + 1 < S:
            x = (xf + mm(weights(1, s), hs[s], NT)).astype(BF)
    g = ct_ref[...]
    for s in reversed(range(S)):
        lsf = ls_ref[s].astype(F32)
        lsf = lsf[:5] + lsf[5:10]
        lrow = jnp.concatenate([lsf[j : j + 1] for j in range(4)] + [lsf[4:5, :64]], axis=1)
        gos[s] = mm(hts[s], g, NT) * lrow
        if s > 0:
            m = mm(weights(0, s), ps[s], NT)
            g = (g.astype(F32) + sts[s : s + 1, :] * m - sts[S + s : S + s + 1, :] * xs[s].astype(F32)).astype(BF)
    acc = jnp.zeros((R, SLICE), F32)
    for s in range(S):
        acc = acc + gos[s] * gos[s]
    tails = []
    for quad in range(2):
        v = [gos[quad * 4 + i].reshape(16, 8, SLICE) for i in range(4)]
        a0, a1 = halves(v[0], v[1])
        b0, b1 = halves(v[2], v[3])
        even = jnp.concatenate([a0, b0], axis=1)
        odd = jnp.concatenate([a1, b1], axis=1)
        mine = jnp.where(is0, even, odd)
        rest = jnp.where(is0, odd, even)
        for t in range(4):
            at = slice(ROWS + 32 * t + 16 * quad, ROWS + 32 * t + 16 * quad + 16)
            gown_ref[:, at] = mine[:, :, t * R : (t + 1) * R].astype(BF)
            goth_ref[:, at] = rest[:, :, t * R : (t + 1) * R].astype(BF)
        tails.append((mine[:, :, 4 * R :], rest[:, :, 4 * R :]))
    gown_ref[:, ROWS + 128 :] = jnp.concatenate([tails[0][0], tails[1][0]], axis=2).astype(BF)
    goth_ref[:, ROWS + 128 :] = jnp.concatenate([tails[0][1], tails[1][1]], axis=2).astype(BF)
    one = jnp.sum(jnp.sum(total, axis=0, keepdims=True), axis=1, keepdims=True)
    two = jnp.sum(jnp.sum(acc, axis=0, keepdims=True), axis=1, keepdims=True)
    norm_ref[...] = jnp.broadcast_to((one + two).reshape(1, 1, 1), (2 * S, 8, R))


def mix_kernel(norm_ref, own_ref, got_ref, out_ref):
    core = lax.axis_index(C)
    sums = [norm_ref[0][:1], norm_ref[1][:1]]
    for k in range(1, S):
        for c in range(2):
            sums[c] = sums[c] + norm_ref[2 * k + c][:1]
    even, odd = (CLIP_NORM / (jnp.sqrt(v) + CLIP_OFFSET) for v in sums)
    mine = jnp.where(core == 0, even, odd)
    other = jnp.where(core == 0, odd, even)
    for i in range(16):
        out_ref[i] = (own_ref[i].astype(F32) * mine + got_ref[i].astype(F32) * other).astype(BF)


def fold(ref, rows):
    total = ref[0, rows].astype(F32)
    for i in range(1, 16):
        total = total + ref[i, rows].astype(F32)
    return total


def sum_out_kernel(got_ref, go_ref):
    go = fold(got_ref, slice(ROWS, 2 * ROWS))
    last = go[4 * 32 :]
    tail = jnp.concatenate([last[:, :64], last[:, 64:]], axis=0)
    go = jnp.concatenate([go[32 * t : 32 * t + 32] for t in range(4)] + [tail], axis=1).reshape(4, 8, SLICE)
    for i in range(4):
        go_ref[2 * i] = go[i]
        go_ref[2 * i + 1] = pltpu.roll(go[i], 4, axis=0)


def sum_in_kernel(got_ref, gi_ref):
    gi_ref[...] = fold(got_ref, slice(0, ROWS)).astype(BF)


def join_kernel(got_ref, out_ref):
    out_ref[0] = jnp.concatenate([got_ref[k, :4] for k in range(S)], axis=1)


def shifted(value, axis, size):
    return [lax.ppermute(value, axis, [(i, (i + d) % size) for i in range(size)]) for d in range(1, size)]


def per_device(inputs, w_in, w_out, layer_scale, cotangent):
    swap = [(0, 1), (1, 0)]
    w1 = w_in[0]
    flops = 2 * T * D * R
    anywhere = pl.BlockSpec(memory_space=pl.ANY)

    w2, pay = call(
        pack_kernel, "pack",
        [((R, D), BF), ((S, 2 * ROWS + 16, R), BF)],
        [anywhere, anywhere, VM],
        [pltpu.VMEM((R, D), BF), pltpu.VMEM((D, R), BF), pltpu.SemaphoreType.DMA((12,))],
        flops=flops // 16, size=4 << 20, vmem=PACK_VMEM,
    )(w1, w_out[0], layer_scale)
    got = lax.all_to_all(pay, Z, 0, 0)

    proj, sq, xt, ct = call(
        project_kernel, "project",
        [((T, 3 * R), BF), ((T, 1), F32), ((SLICE, T), BF), ((SLICE, T), BF)],
        [VM, VM, VM, VM],
        [pltpu.VMEM((5 * R, T), BF)], flops=3 * flops, size=5 << 20, vmem=12,
    )(inputs, cotangent, w1, w2)

    (part,) = call(
        gram_kernel, "gram", [((S, 32 + 3 * T, R), BF)], [VM, VM, VM, VM], flops=flops // 2, size=3 << 20, vmem=12
    )(got, w1, w2, proj)
    part, got = lax.optimization_barrier((part, got))
    part = lax.all_to_all(part, Z, 0, 0)
    own_w = got[:, ROWS : 2 * ROWS]
    ls = got[:, 2 * ROWS :]
    own_w = jnp.stack([own_w] + shifted(own_w, X, 4))
    part, own_w = lax.optimization_barrier((part, own_w))

    kown = lax.all_to_all(jnp.broadcast_to(part[:, :32], (16, S, 32, R)), (Y, X), 0, 0)
    other_w = lax.ppermute(own_w, C, swap)
    kown, other_w = lax.optimization_barrier((kown, other_w))
    koth = lax.ppermute(kown, C, swap)

    gown, goth, norm = call(
        main_kernel, "main",
        [((16, 2 * ROWS, R), BF), ((16, 2 * ROWS, R), BF), ((2 * S, 8, R), F32)],
        [VM, VM, VM, VM, anywhere, anywhere, VM, VM, VM],
        [
            pltpu.VMEM((S * R, S * R), BF),
            pltpu.VMEM((T, S * R), F32),
            pltpu.VMEM((T, S * R), F32),
            pltpu.VMEM((T, S * R), F32),
            pltpu.VMEM((T, S * R), F32),
            pltpu.VMEM((S, T, R), BF),
            pltpu.VMEM((S, R, T), BF),
            pltpu.VMEM((S, T, R), BF),
            pltpu.VMEM((R, T), F32),
            pltpu.VMEM((2, 4, S, QUARTER, R), BF),
            pltpu.VMEM((S, SLICE, T), BF),
            pltpu.VMEM((S, R, SLICE), F32),
            pltpu.SemaphoreType.DMA((8,)),
        ],
        flops=2 * 32 * SLICE * T * R + 2 * 192 * T * R * R, size=10 << 20, trans=S * T * R, vmem=28,
    )(kown, koth, part, sq, own_w, other_w, xt, ct, ls)

    ggot = lax.ppermute(goth, C, swap)
    norm = lax.all_to_all(norm, (Z, C), 0, 0)
    (both,) = call(mix_kernel, "mix", [((16, 2 * ROWS, R), BF)], [VM, VM, VM], size=4 << 20)(norm, gown, ggot)
    both = lax.all_to_all(both, (Y, X), 0, 0)
    (go,) = call(sum_out_kernel, "sum_out", [((S, 8, SLICE), F32)], [VM], size=1 << 20)(both)
    go = lax.all_to_all(go, Z, 0, 0)
    (gi,) = call(sum_in_kernel, "sum_in", [((ROWS, R), BF)], [VM], size=1 << 20)(both)
    route = [(k * 32 + s * 4 + j, s * 32 + k * 4 + j) for k in range(S) for s in range(S) for j in range(4)]
    grad_in = lax.ppermute(gi, (Z, Y, X, C), route).astype(F32)[None]
    (grad_out,) = call(join_kernel, "join", [((1, 4, D), F32)], [VM])(go)
    return grad_in, grad_out


def solution(mesh):
    split = Mesh(np.asarray(mesh.devices).reshape(S, 4, 4, 2), (Z, Y, X, C))
    dp = (Y, X, C)
    return jax.shard_map(
        per_device,
        mesh=split,
        in_specs=(P(dp, None), P(Z, None, None), P(Z, None, None), P(Z, None), P(dp, None)),
        out_specs=(P(Z, dp, None), P(Z, dp, None)),
        check_vma=False,
    )
```

```python
import jax
import jax.numpy as jnp
import numpy as np
from jax import lax
from jax.experimental import pallas as pl
from jax.experimental.pallas import tpu as pltpu
from jax.sharding import Mesh, PartitionSpec as P

EPS = 1e-06
CLIP_NORM = 256.0
CLIP_OFFSET = 0.01
S = 8
R = 128
T = 128
D = 4608
SLICE = D // S
QUARTER = SLICE // 4
PACK_VMEM = 56
DIRECT = 6
TAIL_FLOPS = 20 * 10**9
Z, Y, X, C = "section", "y", "x", "core"
BF = jnp.bfloat16
F32 = jnp.float32
NN = (((1,), (0,)), ((), ()))
NT = (((1,), (1,)), ((), ()))
GELU_A = 0.7978845608028654
GELU_B = 0.044715
HALF = D // 2
ROWS = D * 4 // R
VM = pl.BlockSpec(memory_space=pltpu.VMEM)
SPREAD = VM


def mm(a, b, dims=NN):
    return lax.dot_general(a, b, dims, preferred_element_type=F32)


def halves(even, odd):
    low = lax.broadcasted_iota(jnp.int32, even.shape, 1) < 4
    return (
        jnp.where(low, even, pltpu.roll(odd, 4, axis=1)),
        jnp.where(low, pltpu.roll(even, 4, axis=1), odd),
    )


def call(kernel, name, outs, ins, scratch=(), flops=0, size=1 << 21, trans=0, vmem=8, to=None, alias=None):
    return pl.pallas_call(
        kernel,
        out_shape=tuple(jax.ShapeDtypeStruct(*o) for o in outs),
        in_specs=list(ins),
        out_specs=tuple(to or [VM] * len(outs)),
        scratch_shapes=list(scratch),
        input_output_aliases=alias or {},
        compiler_params=pltpu.CompilerParams(vmem_limit_bytes=vmem << 20),
        cost_estimate=pl.CostEstimate(flops=flops, bytes_accessed=size, transcendentals=trans),
        name=name,
    )


def pack_kernel(w_in_ref, w_out_ref, ls_ref, pay_ref, rows, wide, turned, strip, sem):
    y, x, core = lax.axis_index(Y), lax.axis_index(X), lax.axis_index(C)
    q = (x * 2 + core) * 4 + y
    row_copy = pltpu.make_async_copy(w_out_ref.at[pl.ds(pl.multiple_of((q // 4) * 16, 16), 16)], rows, sem.at[0])
    row_copy.start()
    first = [SLICE * k + QUARTER * x for k in range(S)]

    def in_copies():
        return [
            pltpu.make_async_copy(
                w_in_ref.at[pl.ds(pl.multiple_of(first[k], 16), QUARTER)],
                pay_ref.at[k, pl.ds(ROWS, QUARTER)] if k < DIRECT else turned.at[k, pl.ds(0, QUARTER)],
                sem.at[1 + k],
            )
            for k in range(S)
        ]

    def out_copies():
        return [
            pltpu.make_async_copy(
                w_out_ref.at[:, pl.ds(pl.multiple_of((first[k] // R) * R, R), 2 * R)], wide.at[k], sem.at[1 + k]
            )
            for k in range(S)
        ]

    @pl.when(core == 0)
    def _():
        for cp in in_copies():
            cp.start()

    @pl.when(core != 0)
    def _():
        for cp in out_copies():
            cp.start()

    row_copy.wait()
    block = rows[...].astype(F32) * ls_ref[...]
    group = q % 4
    mine = jnp.where(group < 2, block[:8], block[8:])
    turn = pltpu.roll(mine, 4, axis=0)
    odd = group % 2 == 1
    low = lax.broadcasted_iota(jnp.int32, (8, HALF), 0) < 4
    mine = jnp.where(
        low,
        jnp.where(odd, turn[:, :HALF], mine[:, :HALF]),
        jnp.where(odd, mine[:, HALF:], turn[:, HALF:]),
    )
    for u in range(9):
        two = jnp.concatenate([mine[:, 256 * u : 256 * u + R], mine[:, 256 * u + R : 256 * (u + 1)]], axis=0)
        strip[16 * u : 16 * u + 16] = two.astype(BF)
    sends = [pltpu.make_async_copy(strip, pay_ref.at[k, pl.ds(0, ROWS)], sem.at[9 + k]) for k in range(S)]
    for cp in sends:
        cp.start()

    @pl.when(core == 0)
    def _():
        copies = in_copies()
        outs = []
        for k in range(DIRECT, S):
            copies[k].wait()
            out = pltpu.make_async_copy(turned.at[k, pl.ds(0, QUARTER)], pay_ref.at[k, pl.ds(ROWS, QUARTER)], sem.at[17 + k])
            out.start()
            outs.append(out)
        for cp in copies[:DIRECT] + outs:
            cp.wait()

    @pl.when(core != 0)
    def _():
        copies = []
        for k, cp in enumerate(out_copies()):
            cp.wait()
            base = pl.multiple_of((first[k] // R) * R, R)
            for i in range(2):
                part = wide[k, :, i * R : (i + 1) * R].astype(F32) * ls_ref[:, pl.ds(base + i * R, R)]
                turned[k, i * R : (i + 1) * R, :] = part.T.astype(BF)
            start = pl.multiple_of(first[k] % R, 16)
            out = pltpu.make_async_copy(turned.at[k, pl.ds(start, QUARTER)], pay_ref.at[k, pl.ds(ROWS, QUARTER)], sem.at[17 + k])
            out.start()
            copies.append(out)
        for out in copies:
            out.wait()

    for cp in sends:
        cp.wait()


def project_kernel(x_ref, c_ref, w_in_ref, w_out_ref, ls_ref, proj, scales, sq_ref, xt_ref, ct_ref, wide):
    z = lax.axis_index(Z)
    xv = x_ref[...]
    ls = ls_ref[...]
    w2 = (w_out_ref[...].astype(F32) * ls).astype(BF)
    proj[:T] = mm(xv, w_in_ref[...]).astype(BF)
    proj[T : 2 * T] = mm(xv, w2, NT).astype(BF)
    proj[2 * T :] = mm(c_ref[...], w2, NT).astype(BF)
    top = ls.astype(BF).astype(F32)
    low_part = ls - top
    for k in range(S):
        lines = []
        for part in (top, low_part):
            lines += [part[:, SLICE * k + R * j : SLICE * k + R * (j + 1)] for j in range(4)]
            tail = part[:, SLICE * k + 512 : SLICE * (k + 1)]
            lines.append(jnp.concatenate([tail, tail], axis=1))
        lines.append(jnp.zeros((6, R), F32))
        scales[k] = jnp.concatenate(lines, axis=0).astype(BF)
    xf = xv.astype(F32)
    sq_ref[...] = jnp.sum(xf * xf, axis=1, keepdims=True)
    base = pl.multiple_of(((z * 9) // 2) * R, R)
    off = pl.multiple_of((z % 2) * 64, 16)
    for src, dst in ((x_ref, xt_ref), (c_ref, ct_ref)):
        for t in range(5):
            wide[t * R : (t + 1) * R, :] = src[:, pl.ds(base + t * R, R)].astype(F32).T.astype(BF)
        dst[...] = wide[pl.ds(off, SLICE), :]


def gram_kernel(got_ref, w_in_ref, w_out_ref, ls_ref, proj_ref, scales_ref, out_ref, row, sem):
    z = lax.axis_index(Z)
    copies = [pltpu.make_async_copy(proj_ref, out_ref.at[k, pl.ds(32, 3 * T)], sem.at[k]) for k in range(S)]
    copies.append(pltpu.make_async_copy(scales_ref, out_ref.at[:, pl.ds(32 + 3 * T, 16)], sem.at[S]))
    for cp in copies:
        cp.start()
    ls = ls_ref[...]
    first, second = [], []
    for u in range(9):
        block = got_ref[:, 16 * u : 16 * u + 16, :].astype(F32)
        for part in (block[:, :8], block[:, 8:]):
            part = part.reshape(4, 2, 8, R)
            a, b = halves(part[:, 0], part[:, 1])
            first.append(a.reshape(32, R).astype(BF))
            second.append(b.reshape(32, R).astype(BF))
    first = jnp.concatenate(first, axis=1)
    second = jnp.concatenate(second, axis=1)
    up = mm(first, w_in_ref[:HALF]) + mm(second, w_in_ref[HALF:])
    down = mm((first.astype(F32) * ls[:, :HALF]).astype(BF), w_out_ref[:, :HALF], NT)
    down = down + mm((second.astype(F32) * ls[:, HALF:]).astype(BF), w_out_ref[:, HALF:], NT)
    below = (lax.broadcasted_iota(jnp.int32, (32, R), 0) // 4) < z
    out = jnp.where(below, up, down).astype(BF)
    row[...] = out
    sends = [pltpu.make_async_copy(row, out_ref.at[k, pl.ds(0, 32)], sem.at[S + 1 + k]) for k in range(S)]
    for cp in sends:
        cp.start()
    for cp in copies + sends:
        cp.wait()


def spread_kernel(part_ref, out_ref, sem):
    copies = [pltpu.make_async_copy(part_ref.at[:, pl.ds(0, 32)], out_ref.at[i], sem.at[i]) for i in range(16)]
    for cp in copies:
        cp.start()
    for cp in copies:
        cp.wait()


def main_kernel(own_ref, oth_ref, *refs):
    proj_ref, sq_ref, wown_ref, woth_ref, xt_ref, ct_ref, gown_ref, goth_ref, norm_ref = refs[:9]
    kmat, pre, qacc, hacc, slope, hs, hts, ps, sts, wbuf, xs, gos, sem = refs[9:]
    core = lax.axis_index(C)
    is0 = core == 0
    copies = []
    for i in range(4):
        slot = (lax.axis_index(X) + 4 - i) % 4
        for n, (ref, half) in enumerate(((wown_ref, core), (woth_ref, 1 - core))):
            copies.append(pltpu.make_async_copy(ref.at[i], wbuf.at[half, slot], sem.at[i * 2 + n]))
    for cp in copies:
        cp.start()

    def place(s, carry):
        cols = pl.ds(pl.multiple_of(s * R, R), R)
        for x in range(4):
            own = [own_ref[y * 4 + x, s].astype(F32).reshape(4, 8, R) for y in range(4)]
            oth = [oth_ref[y * 4 + x, s].astype(F32).reshape(4, 8, R) for y in range(4)]
            for c in range(2):
                v = [jnp.where(is0, a, b) if c == 0 else jnp.where(is0, b, a) for a, b in zip(own, oth)]
                e01, o01 = halves(v[0], v[1])
                e23, o23 = halves(v[2], v[3])
                ev = jnp.concatenate([e01, e23], axis=1).astype(BF)
                od = jnp.concatenate([o01, o23], axis=1).astype(BF)
                for i in range(4):
                    row = (x * 2 + c) * 16
                    kmat[2 * i * R + row : 2 * i * R + row + 16, cols] = ev[i]
                    kmat[(2 * i + 1) * R + row : (2 * i + 1) * R + row + 16, cols] = od[i]
        return carry

    lax.fori_loop(0, S, place, 0)
    for s in range(S):
        for i, acc in enumerate((pre, qacc, hacc)):
            acc[:, s * R : (s + 1) * R] = proj_ref[s, 32 + T * i : 32 + T * (i + 1)].astype(F32)
    sq = sq_ref[...]
    lane = lax.broadcasted_iota(jnp.int32, (T, R), 1)
    scal = jnp.zeros((T, R), F32)
    inv = []
    for s in range(S):
        here = slice(s * R, (s + 1) * R)
        r = lax.rsqrt(sq * (1.0 / D) + EPS)
        inv.append(r)
        scal = jnp.where(lane == s, r, scal)
        v = pre[:, here] * r
        pre[:, here] = v
        th = jnp.tanh(GELU_A * (v + GELU_B * v * v * v))
        h = (0.5 * v * (1.0 + th)).astype(BF)
        slope[:, here] = 0.5 * (1.0 + th) + 0.5 * v * (1.0 - th * th) * (GELU_A * (1.0 + 3.0 * GELU_B * v * v))
        hs[s] = h
        hf = h.astype(F32)
        hts[s] = hf.T.astype(BF)
        if s + 1 < S:
            before = qacc[:, here]
            qacc[:, s * R :] += mm(h, kmat[s * R :, here], NT)
            sq = sq + jnp.sum(hf * (before + qacc[:, here]), axis=1, keepdims=True)
            pre[:, (s + 1) * R :] += mm(h, kmat[here, (s + 1) * R :])
    gam = jnp.zeros((T, 1), F32)
    for s in reversed(range(S)):
        here = slice(s * R, (s + 1) * R)
        hg = hacc[:, here]
        if s + 1 < S:
            hg = hg - gam * qacc[:, here]
        p = (hg * slope[:, here]).astype(BF)
        ps[s] = p
        r = inv[s]
        cen = r * r * (jnp.sum(p.astype(F32) * pre[:, here], axis=1, keepdims=True) * (1.0 / D))
        scal = jnp.where(lane == S + s, cen, scal)
        if s > 0:
            upd = r * mm(p, kmat[: s * R, here], NT)
            if s + 1 < S:
                upd = upd - gam * mm(hs[s], kmat[here, : s * R])
            hacc[:, : s * R] += upd
        gam = gam + cen
    sts[...] = scal.T
    for cp in copies:
        cp.wait()

    def weights(kind, s):
        return wbuf[kind, :, s].reshape(SLICE, R)

    total = jnp.zeros((QUARTER, R), F32)
    x = xt_ref[...]
    for s in range(S):
        xs[s] = x
        xf = x.astype(F32)
        n = (xf * sts[s : s + 1, :]).astype(BF)
        gi = mm(n, ps[s])
        for j1 in range(2):
            a = gi[2 * j1 * QUARTER : (2 * j1 + 1) * QUARTER]
            b = gi[(2 * j1 + 1) * QUARTER : (2 * j1 + 2) * QUARTER]
            total = total + a * a + b * b
            gown_ref[s * 2 + j1, :ROWS] = jnp.where(is0, a, b).astype(BF)
            goth_ref[s * 2 + j1, :ROWS] = jnp.where(is0, b, a).astype(BF)
        if s + 1 < S:
            x = (xf + mm(weights(1, s), hs[s], NT)).astype(BF)
    g = ct_ref[...]
    for s in reversed(range(S)):
        lsf = proj_ref[s, 32 + 3 * T :].astype(F32)
        lsf = lsf[:5] + lsf[5:10]
        lrow = jnp.concatenate([lsf[j : j + 1] for j in range(4)] + [lsf[4:5, :64]], axis=1)
        gos[s] = mm(hts[s], g, NT) * lrow
        if s > 0:
            m = mm(weights(0, s), ps[s], NT)
            g = (g.astype(F32) + sts[s : s + 1, :] * m - sts[S + s : S + s + 1, :] * xs[s].astype(F32)).astype(BF)
    acc = jnp.zeros((R, SLICE), F32)
    for s in range(S):
        acc = acc + gos[s] * gos[s]
    tails = []
    for quad in range(2):
        v = [gos[quad * 4 + i].reshape(16, 8, SLICE) for i in range(4)]
        a0, a1 = halves(v[0], v[1])
        b0, b1 = halves(v[2], v[3])
        even = jnp.concatenate([a0, b0], axis=1)
        odd = jnp.concatenate([a1, b1], axis=1)
        mine = jnp.where(is0, even, odd)
        rest = jnp.where(is0, odd, even)
        for t in range(4):
            at = slice(ROWS + 32 * t + 16 * quad, ROWS + 32 * t + 16 * quad + 16)
            gown_ref[:, at] = mine[:, :, t * R : (t + 1) * R].astype(BF)
            goth_ref[:, at] = rest[:, :, t * R : (t + 1) * R].astype(BF)
        tails.append((mine[:, :, 4 * R :], rest[:, :, 4 * R :]))
    gown_ref[:, ROWS + 128 :] = jnp.concatenate([tails[0][0], tails[1][0]], axis=2).astype(BF)
    goth_ref[:, ROWS + 128 :] = jnp.concatenate([tails[0][1], tails[1][1]], axis=2).astype(BF)
    one = jnp.sum(jnp.sum(total, axis=0, keepdims=True), axis=1, keepdims=True)
    two = jnp.sum(jnp.sum(acc, axis=0, keepdims=True), axis=1, keepdims=True)
    norm_ref[...] = jnp.broadcast_to((one + two).reshape(1, 1, 1), (2 * S, 8, R))


def mix_kernel(norm_ref, own_ref, got_ref, out_ref):
    core = lax.axis_index(C)
    sums = [norm_ref[0][:1], norm_ref[1][:1]]
    for k in range(1, S):
        for c in range(2):
            sums[c] = sums[c] + norm_ref[2 * k + c][:1]
    even, odd = (CLIP_NORM / (jnp.sqrt(v) + CLIP_OFFSET) for v in sums)
    mine = jnp.where(core == 0, even, odd)
    other = jnp.where(core == 0, odd, even)
    for i in range(16):
        out_ref[i] = (own_ref[i].astype(F32) * mine + got_ref[i].astype(F32) * other).astype(BF)


def fold(ref, rows):
    total = ref[0, rows].astype(F32)
    for i in range(1, 16):
        total = total + ref[i, rows].astype(F32)
    return total


def sum_out_kernel(got_ref, go_ref):
    go = fold(got_ref, slice(ROWS, 2 * ROWS))
    last = go[4 * 32 :]
    tail = jnp.concatenate([last[:, :64], last[:, 64:]], axis=0)
    go = jnp.concatenate([go[32 * t : 32 * t + 32] for t in range(4)] + [tail], axis=1).reshape(4, 8, SLICE)
    for i in range(4):
        go_ref[2 * i] = go[i][:4].astype(BF)
        go_ref[2 * i + 1] = go[i][4:].astype(BF)


def sum_in_kernel(got_ref, gi_ref):
    gi_ref[...] = fold(got_ref, slice(0, ROWS)).astype(BF)


def join_kernel(got_ref, gi_ref, out_ref, in_ref):
    in_ref[0] = gi_ref[...].astype(F32)
    out_ref[0] = jnp.concatenate([got_ref[k].astype(F32) for k in range(S)], axis=1)


def shifted(value, axis, size):
    return [lax.ppermute(value, axis, [(i, (i + d) % size) for i in range(size)]) for d in range(1, size)]


def per_device(inputs, w_in, w_out, layer_scale, cotangent):
    swap = [(0, 1), (1, 0)]
    w1 = w_in[0]
    flops = 2 * T * D * R
    anywhere = pl.BlockSpec(memory_space=pl.ANY)

    far = pl.BlockSpec(memory_space=pltpu.HBM)
    (pay,) = call(
        pack_kernel, "pack",
        [((S, 2 * ROWS, R), BF)],
        [anywhere, anywhere, VM],
        [
            pltpu.VMEM((16, D), BF),
            pltpu.VMEM((S, R, 2 * R), BF),
            pltpu.VMEM((S, 2 * R, R), BF),
            pltpu.VMEM((ROWS, R), BF),
            pltpu.SemaphoreType.DMA((25,)),
        ],
        flops=flops // 16, size=2 << 20, vmem=PACK_VMEM, to=[far],
    )(w1, w_out[0], layer_scale)
    got = lax.all_to_all(pay, Z, 0, 0)

    proj, scales, sq, xt, ct = call(
        project_kernel, "project",
        [((3 * T, R), BF), ((S, 16, R), BF), ((T, 1), F32), ((SLICE, T), BF), ((SLICE, T), BF)],
        [VM, VM, VM, VM, VM],
        [pltpu.VMEM((5 * R, T), BF)], flops=3 * flops, size=5 << 20, vmem=12,
    )(inputs, cotangent, w1, w_out[0], layer_scale)

    (part,) = call(
        gram_kernel, "gram", [((S, 48 + 3 * T, R), BF)], [VM] * 6,
        [pltpu.VMEM((32, R), BF), pltpu.SemaphoreType.DMA((2 * S + 1,))],
        flops=flops // 2, size=3 << 20, vmem=12, to=[far],
    )(got, w1, w_out[0], layer_scale, proj, scales)
    part, got = lax.optimization_barrier((part, got))
    part = lax.all_to_all(part, Z, 0, 0)
    own_w = got[:, ROWS : 2 * ROWS]
    own_w = jnp.stack([own_w] + shifted(own_w, X, 4))
    part, own_w = lax.optimization_barrier((part, own_w))

    (spread,) = call(
        spread_kernel, "spread", [((16, S, 32, R), BF)], [VM], [pltpu.SemaphoreType.DMA((16,))], to=[SPREAD]
    )(part)
    kown = lax.all_to_all(spread, (Y, X), 0, 0)
    kown, own_w = lax.optimization_barrier((kown, own_w))
    koth = lax.ppermute(kown, C, swap)
    other_w = lax.ppermute(own_w, C, swap)

    gown, goth, norm = call(
        main_kernel, "main",
        [((16, 2 * ROWS, R), BF), ((16, 2 * ROWS, R), BF), ((2 * S, 8, R), F32)],
        [VM, VM, VM, VM, anywhere, anywhere, VM, VM],
        [
            pltpu.VMEM((S * R, S * R), BF),
            pltpu.VMEM((T, S * R), F32),
            pltpu.VMEM((T, S * R), F32),
            pltpu.VMEM((T, S * R), F32),
            pltpu.VMEM((T, S * R), F32),
            pltpu.VMEM((S, T, R), BF),
            pltpu.VMEM((S, R, T), BF),
            pltpu.VMEM((S, T, R), BF),
            pltpu.VMEM((R, T), F32),
            pltpu.VMEM((2, 4, S, QUARTER, R), BF),
            pltpu.VMEM((S, SLICE, T), BF),
            pltpu.VMEM((S, R, SLICE), F32),
            pltpu.SemaphoreType.DMA((8,)),
        ],
        flops=2 * 32 * SLICE * T * R + 2 * 192 * T * R * R, size=10 << 20, trans=S * T * R, vmem=28,
    )(kown, koth, part, sq, own_w, other_w, xt, ct)

    ggot = lax.ppermute(goth, C, swap)
    norm = lax.all_to_all(norm, (Z, C), 0, 0)
    (both,) = call(mix_kernel, "mix", [((16, 2 * ROWS, R), BF)], [VM, VM, VM], size=4 << 20)(norm, gown, ggot)
    both = lax.all_to_all(both, (Y, X), 0, 0)
    (go_sent,) = call(sum_out_kernel, "sum_out", [((S, 4, SLICE), BF)], [VM], size=1 << 20)(both)
    go = lax.all_to_all(go_sent, Z, 0, 0)
    both, go_sent = lax.optimization_barrier((both, go_sent))
    (gi,) = call(sum_in_kernel, "sum_in", [((ROWS, R), BF)], [VM], flops=TAIL_FLOPS, size=1 << 20)(both)
    route = [(k * 32 + s * 4 + j, s * 32 + k * 4 + j) for k in range(S) for s in range(S) for j in range(4)]
    gi = lax.ppermute(gi, (Z, Y, X, C), route)
    grad_out, grad_in = call(join_kernel, "join", [((1, 4, D), F32), ((1, ROWS, R), F32)], [VM, VM])(go, gi)
    return grad_in, grad_out


def solution(mesh):
    split = Mesh(np.asarray(mesh.devices).reshape(S, 4, 4, 2), (Z, Y, X, C))
    dp = (Y, X, C)
    return jax.shard_map(
        per_device,
        mesh=split,
        in_specs=(P(dp, None), P(Z, None, None), P(Z, None, None), P(Z, None), P(dp, None)),
        out_specs=(P(Z, dp, None), P(Z, dp, None)),
        check_vma=False,
    )
```

```python
import jax
import jax.numpy as jnp
import numpy as np
from jax import lax
from jax.experimental import pallas as pl
from jax.experimental.pallas import tpu as pltpu
from jax.sharding import Mesh, PartitionSpec as P

EPS = 1e-06
CLIP_NORM = 256.0
CLIP_OFFSET = 0.01
S = 8
R = 128
T = 128
D = 4608
SLICE = D // S
QUARTER = SLICE // 4
PACK_VMEM = 56
LATE = 6
BAND = D // 4
Z, Y, X, C = "section", "y", "x", "core"
BF = jnp.bfloat16
F32 = jnp.float32
NN = (((1,), (0,)), ((), ()))
NT = (((1,), (1,)), ((), ()))
GELU_A = 0.7978845608028654
GELU_B = 0.044715
HALF = D // 2
ROWS = D * 4 // R
VM = pl.BlockSpec(memory_space=pltpu.VMEM)
SPREAD = VM


def mm(a, b, dims=NN):
    return lax.dot_general(a, b, dims, preferred_element_type=F32)


def halves(even, odd):
    low = lax.broadcasted_iota(jnp.int32, even.shape, 1) < 4
    return (
        jnp.where(low, even, pltpu.roll(odd, 4, axis=1)),
        jnp.where(low, pltpu.roll(even, 4, axis=1), odd),
    )


def call(kernel, name, outs, ins, scratch=(), flops=0, size=1 << 21, trans=0, vmem=8, to=None, alias=None):
    return pl.pallas_call(
        kernel,
        out_shape=tuple(jax.ShapeDtypeStruct(*o) for o in outs),
        in_specs=list(ins),
        out_specs=tuple(to or [VM] * len(outs)),
        scratch_shapes=list(scratch),
        input_output_aliases=alias or {},
        compiler_params=pltpu.CompilerParams(vmem_limit_bytes=vmem << 20),
        cost_estimate=pl.CostEstimate(flops=flops, bytes_accessed=size, transcendentals=trans),
        name=name,
    )


def swap_units(count, picked=None):
    row = lax.broadcasted_iota(jnp.int32, (count, R), 0)
    col = lax.broadcasted_iota(jnp.int32, (count, R), 1)
    outer = row // 16 if picked is None else picked
    return (col == ((row % 16) // 2) * 16 + outer * 2 + row % 2).astype(BF)


def pack_kernel(w_in_ref, w_out_ref, ls_ref, pay_ref, rows, wide, block, strip, sem):
    y, x, core = lax.axis_index(Y), lax.axis_index(X), lax.axis_index(C)
    q = (x * 2 + core) * 4 + y
    row_copy = pltpu.make_async_copy(w_out_ref.at[pl.ds(pl.multiple_of((q // 4) * 16, 16), 16)], rows, sem.at[0])
    row_copy.start()
    start = pl.multiple_of(x * BAND, R)

    def in_copy():
        return pltpu.make_async_copy(w_in_ref.at[pl.ds(start, BAND)], block, sem.at[1])

    def out_copy():
        return pltpu.make_async_copy(w_out_ref.at[:, pl.ds(start, BAND)], wide, sem.at[1])

    def late_copies():
        return [
            pltpu.make_async_copy(
                w_in_ref.at[pl.ds(pl.multiple_of(start + QUARTER * e + 16 * k, 16), 16)],
                pay_ref.at[k, pl.ds(ROWS + 16 * e, 16)],
                sem.at[2 + S + k * S + e],
            )
            for k in range(LATE)
            for e in range(S)
        ]

    @pl.when(core == 0)
    def _():
        for cp in late_copies():
            cp.start()
        in_copy().start()

    @pl.when(core != 0)
    def _():
        out_copy().start()

    row_copy.wait()
    part = rows[...].astype(F32) * ls_ref[...]
    group = q % 4
    mine = jnp.where(group < 2, part[:8], part[8:])
    turn = pltpu.roll(mine, 4, axis=0)
    odd = group % 2 == 1
    low = lax.broadcasted_iota(jnp.int32, (8, HALF), 0) < 4
    mine = jnp.where(
        low,
        jnp.where(odd, turn[:, :HALF], mine[:, :HALF]),
        jnp.where(odd, mine[:, HALF:], turn[:, HALF:]),
    )
    for u in range(9):
        two = jnp.concatenate([mine[:, 256 * u : 256 * u + R], mine[:, 256 * u + R : 256 * (u + 1)]], axis=0).astype(BF)
        for k in range(S):
            strip[k, 16 * u : 16 * u + 16] = two

    @pl.when(core == 0)
    def _():
        in_copy().wait()

    @pl.when(core != 0)
    def _():
        out_copy().wait()
        scale = ls_ref[:, pl.ds(start, BAND)]
        for t in range(BAND // R):
            tile = wide[:, t * R : (t + 1) * R].astype(F32) * scale[:, t * R : (t + 1) * R]
            block[t * R : (t + 1) * R, :] = tile.T.astype(BF)

    for k in range(S):
        for e in range(S):
            strip[k, ROWS + 16 * e : ROWS + 16 * e + 16] = block[QUARTER * e + 16 * k : QUARTER * e + 16 * k + 16]
    left = jnp.concatenate([block[QUARTER * e + 128 : QUARTER * (e + 1)] for e in range(S)], axis=0)
    left = mm(swap_units(R), left).astype(BF)
    for k in range(S):
        strip[k, ROWS + 128 :] = left[16 * k : 16 * k + 16]

    def sends(late):
        if not late:
            return [pltpu.make_async_copy(strip.at[k], pay_ref.at[k], sem.at[2 + k]) for k in range(S)]
        return [
            pltpu.make_async_copy(strip.at[k, pl.ds(a, n)], pay_ref.at[k, pl.ds(a, n)], sem.at[2 + S + S * LATE + 2 * k + i])
            for k in range(LATE)
            for i, (a, n) in enumerate(((0, ROWS), (ROWS + 128, 16)))
        ] + [pltpu.make_async_copy(strip.at[k], pay_ref.at[k], sem.at[2 + k]) for k in range(LATE, S)]

    @pl.when(core == 0)
    def _():
        for cp in sends(True):
            cp.start()
        for cp in late_copies() + sends(True):
            cp.wait()

    @pl.when(core != 0)
    def _():
        for cp in sends(False):
            cp.start()
        for cp in sends(False):
            cp.wait()


def project_kernel(x_ref, c_ref, w_in_ref, w_out_ref, ls_ref, proj, scales, sq_ref, xt_ref, ct_ref, wide):
    z = lax.axis_index(Z)
    xv = x_ref[...]
    ls = ls_ref[...]
    w2 = (w_out_ref[...].astype(F32) * ls).astype(BF)
    proj[:T] = mm(xv, w_in_ref[...]).astype(BF)
    proj[T : 2 * T] = mm(xv, w2, NT).astype(BF)
    proj[2 * T :] = mm(c_ref[...], w2, NT).astype(BF)
    top = ls.astype(BF).astype(F32)
    low_part = ls - top
    bands = [part[:, BAND * j : BAND * (j + 1)] for part in (top, low_part) for j in range(4)]
    bands = jnp.concatenate(bands, axis=0)
    for k in range(S):
        main = [bands[:, QUARTER * e + 16 * k : QUARTER * e + 16 * k + 16] for e in range(S)]
        rest = [bands[:, QUARTER * e + 128 + 2 * k : QUARTER * e + 130 + 2 * k] for e in range(S)]
        rest = jnp.concatenate(rest + [jnp.zeros((S, R - 16), F32)], axis=1)
        scales[k] = jnp.concatenate([jnp.concatenate(main, axis=1), rest], axis=0).astype(BF)
    xf = xv.astype(F32)
    sq_ref[...] = jnp.sum(xf * xf, axis=1, keepdims=True)
    mine = swap_units(16, z)
    for src, dst in ((x_ref, xt_ref), (c_ref, ct_ref)):
        for t in range(D // R):
            wide[t * R : (t + 1) * R, :] = src[:, t * R : (t + 1) * R].astype(F32).T.astype(BF)
        for j in range(4):
            left = []
            for e in range(S):
                at = BAND * j + QUARTER * e
                dst[R * j + 16 * e : R * j + 16 * e + 16] = wide[pl.ds(pl.multiple_of(at + 16 * z, 16), 16), :]
                left.append(wide[at + 128 : at + QUARTER])
            dst[512 + 16 * j : 512 + 16 * j + 16] = mm(mine, jnp.concatenate(left, axis=0)).astype(BF)


def gram_kernel(got_ref, w_in_ref, w_out_ref, ls_ref, proj_ref, scales_ref, out_ref):
    z = lax.axis_index(Z)
    for k in range(S):
        out_ref[k, 32 : 32 + 3 * T] = proj_ref[...]
        out_ref[k, 32 + 3 * T :] = scales_ref[k]
    ls = ls_ref[...]
    first, second = [], []
    for u in range(9):
        block = got_ref[:, 16 * u : 16 * u + 16, :].astype(F32)
        for part in (block[:, :8], block[:, 8:]):
            part = part.reshape(4, 2, 8, R)
            a, b = halves(part[:, 0], part[:, 1])
            first.append(a.reshape(32, R).astype(BF))
            second.append(b.reshape(32, R).astype(BF))
    first = jnp.concatenate(first, axis=1)
    second = jnp.concatenate(second, axis=1)
    up = mm(first, w_in_ref[:HALF]) + mm(second, w_in_ref[HALF:])
    down = mm((first.astype(F32) * ls[:, :HALF]).astype(BF), w_out_ref[:, :HALF], NT)
    down = down + mm((second.astype(F32) * ls[:, HALF:]).astype(BF), w_out_ref[:, HALF:], NT)
    below = (lax.broadcasted_iota(jnp.int32, (32, R), 0) // 4) < z
    out = jnp.where(below, up, down).astype(BF)
    for k in range(S):
        out_ref[k, :32] = out


def spread_kernel(part_ref, out_ref, sem):
    copies = [pltpu.make_async_copy(part_ref.at[:, pl.ds(0, 32)], out_ref.at[i], sem.at[i]) for i in range(16)]
    for cp in copies:
        cp.start()
    for cp in copies:
        cp.wait()


def main_kernel(own_ref, oth_ref, *refs):
    proj_ref, sq_ref, wown_ref, woth_ref, xt_ref, ct_ref, gown_ref, goth_ref, norm_ref = refs[:9]
    kmat, pre, qacc, hacc, slope, hs, hts, ps, sts, wbuf, xs, gos, lefts, sem = refs[9:]
    core = lax.axis_index(C)
    is0 = core == 0
    copies = []
    for i in range(4):
        slot = (lax.axis_index(X) + 4 - i) % 4
        for n, (ref, half) in enumerate(((wown_ref, core), (woth_ref, 1 - core))):
            copies.append(pltpu.make_async_copy(ref.at[i], wbuf.at[half, slot], sem.at[i * 2 + n]))
    for cp in copies:
        cp.start()

    def place(s, carry):
        cols = pl.ds(pl.multiple_of(s * R, R), R)
        for x in range(4):
            own = [own_ref[y * 4 + x, s].astype(F32).reshape(4, 8, R) for y in range(4)]
            oth = [oth_ref[y * 4 + x, s].astype(F32).reshape(4, 8, R) for y in range(4)]
            for c in range(2):
                v = [jnp.where(is0, a, b) if c == 0 else jnp.where(is0, b, a) for a, b in zip(own, oth)]
                e01, o01 = halves(v[0], v[1])
                e23, o23 = halves(v[2], v[3])
                ev = jnp.concatenate([e01, e23], axis=1).astype(BF)
                od = jnp.concatenate([o01, o23], axis=1).astype(BF)
                for i in range(4):
                    row = (x * 2 + c) * 16
                    kmat[2 * i * R + row : 2 * i * R + row + 16, cols] = ev[i]
                    kmat[(2 * i + 1) * R + row : (2 * i + 1) * R + row + 16, cols] = od[i]
        return carry

    lax.fori_loop(0, S, place, 0)
    for s in range(S):
        for i, acc in enumerate((pre, qacc, hacc)):
            acc[:, s * R : (s + 1) * R] = proj_ref[s, 32 + T * i : 32 + T * (i + 1)].astype(F32)
    sq = sq_ref[...]
    lane = lax.broadcasted_iota(jnp.int32, (T, R), 1)
    scal = jnp.zeros((T, R), F32)
    inv = []
    for s in range(S):
        here = slice(s * R, (s + 1) * R)
        r = lax.rsqrt(sq * (1.0 / D) + EPS)
        inv.append(r)
        scal = jnp.where(lane == s, r, scal)
        v = pre[:, here] * r
        pre[:, here] = v
        th = jnp.tanh(GELU_A * (v + GELU_B * v * v * v))
        h = (0.5 * v * (1.0 + th)).astype(BF)
        slope[:, here] = 0.5 * (1.0 + th) + 0.5 * v * (1.0 - th * th) * (GELU_A * (1.0 + 3.0 * GELU_B * v * v))
        hs[s] = h
        hf = h.astype(F32)
        hts[s] = hf.T.astype(BF)
        if s + 1 < S:
            before = qacc[:, here]
            qacc[:, s * R :] += mm(h, kmat[s * R :, here], NT)
            sq = sq + jnp.sum(hf * (before + qacc[:, here]), axis=1, keepdims=True)
            pre[:, (s + 1) * R :] += mm(h, kmat[here, (s + 1) * R :])
    gam = jnp.zeros((T, 1), F32)
    for s in reversed(range(S)):
        here = slice(s * R, (s + 1) * R)
        hg = hacc[:, here]
        if s + 1 < S:
            hg = hg - gam * qacc[:, here]
        p = (hg * slope[:, here]).astype(BF)
        ps[s] = p
        r = inv[s]
        cen = r * r * (jnp.sum(p.astype(F32) * pre[:, here], axis=1, keepdims=True) * (1.0 / D))
        scal = jnp.where(lane == S + s, cen, scal)
        if s > 0:
            upd = r * mm(p, kmat[: s * R, here], NT)
            if s + 1 < S:
                upd = upd - gam * mm(hs[s], kmat[here, : s * R])
            hacc[:, : s * R] += upd
        gam = gam + cen
    sts[...] = scal.T
    for cp in copies:
        cp.wait()

    def weights(kind, s):
        return jnp.concatenate([wbuf[kind, j, s, :128] for j in range(4)] + [wbuf[kind, j, s, 128:] for j in range(4)], axis=0)

    total = jnp.zeros((64, R), F32)
    x = xt_ref[...]
    for s in range(S):
        xs[s] = x
        xf = x.astype(F32)
        n = (xf * sts[s : s + 1, :]).astype(BF)
        gi = mm(n, ps[s])
        for j in range(9):
            total = total + gi[64 * j : 64 * j + 64] * gi[64 * j : 64 * j + 64]
        for i in range(16):
            a, b = gi[32 * i : 32 * i + 16], gi[32 * i + 16 : 32 * i + 32]
            gown_ref[i, 16 * s : 16 * s + 16] = jnp.where(is0, a, b).astype(BF)
            goth_ref[i, 16 * s : 16 * s + 16] = jnp.where(is0, b, a).astype(BF)
        for j in range(4):
            lefts[j, 16 * s : 16 * s + 16] = gi[512 + 16 * j : 512 + 16 * j + 16].astype(BF)
        if s + 1 < S:
            x = (xf + mm(weights(1, s), hs[s], NT)).astype(BF)
    units = swap_units(R)
    for j in range(4):
        left = mm(units, lefts[j])
        for i in range(4):
            a, b = left[32 * i : 32 * i + 16], left[32 * i + 16 : 32 * i + 32]
            gown_ref[4 * j + i, 128:ROWS] = jnp.where(is0, a, b).astype(BF)
            goth_ref[4 * j + i, 128:ROWS] = jnp.where(is0, b, a).astype(BF)
    g = ct_ref[...]
    for s in reversed(range(S)):
        lsf = proj_ref[s, 32 + 3 * T :].astype(F32)
        lsf = jnp.concatenate([lsf[:4] + lsf[4:8], lsf[8:12] + lsf[12:]], axis=0)
        lrow = jnp.concatenate([lsf[j : j + 1] for j in range(4)] + [lsf[4 + j : 5 + j, :16] for j in range(4)], axis=1)
        gos[s] = mm(hts[s], g, NT) * lrow
        if s > 0:
            m = mm(weights(0, s), ps[s], NT)
            g = (g.astype(F32) + sts[s : s + 1, :] * m - sts[S + s : S + s + 1, :] * xs[s].astype(F32)).astype(BF)
    acc = jnp.zeros((R, SLICE), F32)
    for s in range(S):
        acc = acc + gos[s] * gos[s]
    tails = []
    for quad in range(2):
        v = [gos[quad * 4 + i].reshape(16, 8, SLICE) for i in range(4)]
        a0, a1 = halves(v[0], v[1])
        b0, b1 = halves(v[2], v[3])
        even = jnp.concatenate([a0, b0], axis=1)
        odd = jnp.concatenate([a1, b1], axis=1)
        mine = jnp.where(is0, even, odd)
        rest = jnp.where(is0, odd, even)
        for t in range(4):
            at = slice(ROWS + 32 * t + 16 * quad, ROWS + 32 * t + 16 * quad + 16)
            gown_ref[:, at] = mine[:, :, t * R : (t + 1) * R].astype(BF)
            goth_ref[:, at] = rest[:, :, t * R : (t + 1) * R].astype(BF)
        tails.append((mine[:, :, 4 * R :], rest[:, :, 4 * R :]))
    gown_ref[:, ROWS + 128 :] = jnp.concatenate([tails[0][0], tails[1][0]], axis=2).astype(BF)
    goth_ref[:, ROWS + 128 :] = jnp.concatenate([tails[0][1], tails[1][1]], axis=2).astype(BF)
    one = jnp.sum(jnp.sum(total, axis=0, keepdims=True), axis=1, keepdims=True)
    two = jnp.sum(jnp.sum(acc, axis=0, keepdims=True), axis=1, keepdims=True)
    norm_ref[...] = jnp.broadcast_to((one + two).reshape(1, 1, 1), (2 * S, 8, R))


def mix_kernel(norm_ref, own_ref, got_ref, out_ref):
    core = lax.axis_index(C)
    sums = [norm_ref[0][:1], norm_ref[1][:1]]
    for k in range(1, S):
        for c in range(2):
            sums[c] = sums[c] + norm_ref[2 * k + c][:1]
    even, odd = (CLIP_NORM / (jnp.sqrt(v) + CLIP_OFFSET) for v in sums)
    mine = jnp.where(core == 0, even, odd)
    other = jnp.where(core == 0, odd, even)
    for i in range(16):
        out_ref[i] = (own_ref[i].astype(F32) * mine + got_ref[i].astype(F32) * other).astype(BF)


def sum_kernel(got_ref, out_ref):
    total = got_ref[0].astype(F32)
    for i in range(1, 16):
        total = total + got_ref[i].astype(F32)
    tiles = [total[ROWS + 32 * t : ROWS + 32 * t + 32].reshape(4, 8, R) for t in range(4)]
    last = total[ROWS + 128 :]
    tail = jnp.concatenate([last[:, :64], last[:, 64:]], axis=0)
    tail = jnp.concatenate([tail, jnp.zeros((32, 64), F32)], axis=1).reshape(4, 8, R)
    first = halves(tiles[0], tiles[1])
    second = halves(tiles[2], tiles[3])
    third = (tail, pltpu.roll(tail, 4, axis=1))
    for s in range(S):
        left = total[128 + 8 * (s // 4) : 136 + 8 * (s // 4)]
        if s % 4:
            left = pltpu.roll(left, 8 - 2 * (s % 4), axis=0)
        parts = [total[16 * s : 16 * s + 16]] + [v[s % 2][s // 2] for v in (first, second, third)] + [left]
        out_ref[s] = jnp.concatenate(parts, axis=0).astype(BF)


def join_kernel(got_ref, out_ref, in_ref):
    row = lax.broadcasted_iota(jnp.int32, (8, R), 0)
    mains, rests, left = [], [], [None, None]
    for k in range(S):
        got = got_ref[k].astype(F32)
        in_ref[0, 16 * k : 16 * k + 16] = got[:16]
        unit = got[40:]
        if k % 4:
            unit = pltpu.roll(unit, 2 * (k % 4), axis=0)
        left[k // 4] = unit if k % 4 == 0 else jnp.where(row // 2 == k % 4, unit, left[k // 4])
        mains.append(got[16:32])
        tail = jnp.concatenate([got[32:36, 16 * j : 16 * j + 16] for j in range(4)], axis=0)
        rests.append(tail)
    in_ref[0, 128:136] = left[0]
    in_ref[0, 136:] = left[1]
    pieces = []
    for e in range(S):
        pieces += [v[:, 16 * e : 16 * e + 16] for v in mains]
        pieces += [v[:, 2 * e : 2 * e + 2] for v in rests]
    whole = jnp.concatenate(pieces, axis=1)
    for j in range(4):
        out_ref[0, :, BAND * j : BAND * (j + 1)] = whole[4 * j : 4 * j + 4]


def shifted(value, axis, size):
    return [lax.ppermute(value, axis, [(i, (i + d) % size) for i in range(size)]) for d in range(1, size)]


def per_device(inputs, w_in, w_out, layer_scale, cotangent):
    swap = [(0, 1), (1, 0)]
    w1 = w_in[0]
    flops = 2 * T * D * R
    anywhere = pl.BlockSpec(memory_space=pl.ANY)

    far = pl.BlockSpec(memory_space=pltpu.HBM)
    (pay,) = call(
        pack_kernel, "pack",
        [((S, 2 * ROWS, R), BF)],
        [anywhere, anywhere, VM],
        [
            pltpu.VMEM((16, D), BF),
            pltpu.VMEM((R, BAND), BF),
            pltpu.VMEM((BAND, R), BF),
            pltpu.VMEM((S, 2 * ROWS, R), BF),
            pltpu.SemaphoreType.DMA((2 + 3 * S + S * S,)),
        ],
        flops=flops // 16, size=2 << 20, vmem=PACK_VMEM, to=[far],
    )(w1, w_out[0], layer_scale)
    got = lax.all_to_all(pay, Z, 0, 0)

    proj, scales, sq, xt, ct = call(
        project_kernel, "project",
        [((3 * T, R), BF), ((S, 16, R), BF), ((T, 1), F32), ((SLICE, T), BF), ((SLICE, T), BF)],
        [VM, VM, VM, VM, VM],
        [pltpu.VMEM((D, T), BF)], flops=3 * flops, size=5 << 20, vmem=16,
    )(inputs, cotangent, w1, w_out[0], layer_scale)

    (part,) = call(
        gram_kernel, "gram", [((S, 48 + 3 * T, R), BF)], [VM] * 6,
        flops=flops // 2, size=3 << 20, vmem=12,
    )(got, w1, w_out[0], layer_scale, proj, scales)
    part, got = lax.optimization_barrier((part, got))
    part = lax.all_to_all(part, Z, 0, 0)
    own_w = got[:, ROWS : 2 * ROWS]
    own_w = jnp.stack([own_w] + shifted(own_w, X, 4))
    part, own_w = lax.optimization_barrier((part, own_w))

    (spread,) = call(
        spread_kernel, "spread", [((16, S, 32, R), BF)], [VM], [pltpu.SemaphoreType.DMA((16,))], to=[SPREAD]
    )(part)
    kown = lax.all_to_all(spread, (Y, X), 0, 0)
    kown, own_w = lax.optimization_barrier((kown, own_w))
    koth = lax.ppermute(kown, C, swap)
    other_w = lax.ppermute(own_w, C, swap)

    gown, goth, norm = call(
        main_kernel, "main",
        [((16, 2 * ROWS, R), BF), ((16, 2 * ROWS, R), BF), ((2 * S, 8, R), F32)],
        [VM, VM, VM, VM, anywhere, anywhere, VM, VM],
        [
            pltpu.VMEM((S * R, S * R), BF),
            pltpu.VMEM((T, S * R), F32),
            pltpu.VMEM((T, S * R), F32),
            pltpu.VMEM((T, S * R), F32),
            pltpu.VMEM((T, S * R), F32),
            pltpu.VMEM((S, T, R), BF),
            pltpu.VMEM((S, R, T), BF),
            pltpu.VMEM((S, T, R), BF),
            pltpu.VMEM((R, T), F32),
            pltpu.VMEM((2, 4, S, QUARTER, R), BF),
            pltpu.VMEM((S, SLICE, T), BF),
            pltpu.VMEM((S, R, SLICE), F32),
            pltpu.VMEM((4, R, R), BF),
            pltpu.SemaphoreType.DMA((8,)),
        ],
        flops=2 * 32 * SLICE * T * R + 2 * 192 * T * R * R, size=10 << 20, trans=S * T * R, vmem=28,
    )(kown, koth, part, sq, own_w, other_w, xt, ct)

    ggot = lax.ppermute(goth, C, swap)
    norm = lax.all_to_all(norm, (Z, C), 0, 0)
    (both,) = call(mix_kernel, "mix", [((16, 2 * ROWS, R), BF)], [VM, VM, VM], size=4 << 20)(norm, gown, ggot)
    both = lax.all_to_all(both, (Y, X), 0, 0)
    (sent,) = call(sum_kernel, "sum", [((S, 48, R), BF)], [VM], size=2 << 20)(both)
    got = lax.all_to_all(sent, Z, 0, 0)
    grad_out, grad_in = call(join_kernel, "join", [((1, 4, D), F32), ((1, ROWS, R), F32)], [VM])(got)
    return grad_in, grad_out


def solution(mesh):
    split = Mesh(np.asarray(mesh.devices).reshape(S, 4, 4, 2), (Z, Y, X, C))
    dp = (Y, X, C)
    return jax.shard_map(
        per_device,
        mesh=split,
        in_specs=(P(dp, None), P(Z, None, None), P(Z, None, None), P(Z, None), P(dp, None)),
        out_specs=(P(Z, dp, None), P(Z, dp, None)),
        check_vma=False,
    )
```

```python
import jax
import jax.numpy as jnp
import numpy as np
from jax import lax
from jax.experimental import pallas as pl
from jax.experimental.pallas import tpu as pltpu
from jax.sharding import Mesh, PartitionSpec as P

EPS = 1e-06
CLIP_NORM = 256.0
CLIP_OFFSET = 0.01
S = 8
R = 128
T = 128
D = 4608
SLICE = D // S
QUARTER = SLICE // 4
PACK_VMEM = 56
LATE = 6
BAND = D // 4
LAST = 2 + 2 * S + S * S
Z, Y, X, C = "section", "y", "x", "core"
BF = jnp.bfloat16
F32 = jnp.float32
NN = (((1,), (0,)), ((), ()))
NT = (((1,), (1,)), ((), ()))
GELU_A = 0.7978845608028654
GELU_B = 0.044715
HALF = D // 2
ROWS = D * 4 // R
VM = pl.BlockSpec(memory_space=pltpu.VMEM)
SPREAD = VM


def mm(a, b, dims=NN):
    return lax.dot_general(a, b, dims, preferred_element_type=F32)


def halves(even, odd):
    low = lax.broadcasted_iota(jnp.int32, even.shape, 1) < 4
    return (
        jnp.where(low, even, pltpu.roll(odd, 4, axis=1)),
        jnp.where(low, pltpu.roll(even, 4, axis=1), odd),
    )


def call(kernel, name, outs, ins, scratch=(), flops=0, size=1 << 21, trans=0, vmem=8, to=None, alias=None):
    return pl.pallas_call(
        kernel,
        out_shape=tuple(jax.ShapeDtypeStruct(*o) for o in outs),
        in_specs=list(ins),
        out_specs=tuple(to or [VM] * len(outs)),
        scratch_shapes=list(scratch),
        input_output_aliases=alias or {},
        compiler_params=pltpu.CompilerParams(vmem_limit_bytes=vmem << 20),
        cost_estimate=pl.CostEstimate(flops=flops, bytes_accessed=size, transcendentals=trans),
        name=name,
    )


def swap_units(count, picked=None):
    row = lax.broadcasted_iota(jnp.int32, (count, R), 0)
    col = lax.broadcasted_iota(jnp.int32, (count, R), 1)
    outer = row // 16 if picked is None else picked
    return (col == ((row % 16) // 2) * 16 + outer * 2 + row % 2).astype(BF)


def pack_kernel(w_in_ref, w_out_ref, far_ls_ref, pay_ref, rows, wide, block, strip, head, ls_ref, sem):
    y, x, core = lax.axis_index(Y), lax.axis_index(X), lax.axis_index(C)
    q = (x * 2 + core) * 4 + y
    row_copy = pltpu.make_async_copy(w_out_ref.at[pl.ds(pl.multiple_of((q // 4) * 16, 16), 16)], rows, sem.at[0])
    row_copy.start()
    ls_copy = pltpu.make_async_copy(far_ls_ref, ls_ref, sem.at[LAST])
    ls_copy.start()
    start = pl.multiple_of(x * BAND, R)

    def in_copy():
        return pltpu.make_async_copy(w_in_ref.at[pl.ds(start, BAND)], block, sem.at[1])

    def out_copy():
        return pltpu.make_async_copy(w_out_ref.at[:, pl.ds(start, BAND)], wide, sem.at[1])

    def late_copies():
        return [
            pltpu.make_async_copy(
                w_in_ref.at[pl.ds(pl.multiple_of(start + QUARTER * e + 16 * k, 16), 16)],
                pay_ref.at[k, pl.ds(ROWS + 16 * e, 16)],
                sem.at[2 + S + k * S + e],
            )
            for k in range(LATE)
            for e in range(S)
        ]

    @pl.when(core == 0)
    def _():
        for cp in late_copies():
            cp.start()
        in_copy().start()

    @pl.when(core != 0)
    def _():
        out_copy().start()

    ls_copy.wait()
    row_copy.wait()
    part = rows[...].astype(F32) * ls_ref[...]
    group = q % 4
    mine = jnp.where(group < 2, part[:8], part[8:])
    turn = pltpu.roll(mine, 4, axis=0)
    odd = group % 2 == 1
    low = lax.broadcasted_iota(jnp.int32, (8, HALF), 0) < 4
    mine = jnp.where(
        low,
        jnp.where(odd, turn[:, :HALF], mine[:, :HALF]),
        jnp.where(odd, mine[:, HALF:], turn[:, HALF:]),
    )
    for u in range(9):
        two = jnp.concatenate([mine[:, 256 * u : 256 * u + R], mine[:, 256 * u + R : 256 * (u + 1)]], axis=0).astype(BF)
        head[16 * u : 16 * u + 16] = two
    heads = [pltpu.make_async_copy(head, pay_ref.at[k, pl.ds(0, ROWS)], sem.at[2 + k]) for k in range(S)]
    for cp in heads:
        cp.start()

    @pl.when(core == 0)
    def _():
        in_copy().wait()

    @pl.when(core != 0)
    def _():
        out_copy().wait()
        scale = ls_ref[:, pl.ds(start, BAND)]
        for t in range(BAND // R):
            tile = wide[:, t * R : (t + 1) * R].astype(F32) * scale[:, t * R : (t + 1) * R]
            block[t * R : (t + 1) * R, :] = tile.T.astype(BF)

    for k in range(S):
        for e in range(S):
            strip[k, 16 * e : 16 * e + 16] = block[QUARTER * e + 16 * k : QUARTER * e + 16 * k + 16]
    left = jnp.concatenate([block[QUARTER * e + 128 : QUARTER * (e + 1)] for e in range(S)], axis=0)
    left = mm(swap_units(R), left).astype(BF)
    for k in range(S):
        strip[k, 128:] = left[16 * k : 16 * k + 16]

    def sends(late):
        return [
            pltpu.make_async_copy(strip.at[k, pl.ds(128, 16)], pay_ref.at[k, pl.ds(ROWS + 128, 16)], sem.at[2 + S + S * S + k])
            if late and k < LATE
            else pltpu.make_async_copy(strip.at[k], pay_ref.at[k, pl.ds(ROWS, ROWS)], sem.at[2 + S + S * S + k])
            for k in range(S)
        ]

    @pl.when(core == 0)
    def _():
        for cp in sends(True):
            cp.start()
        for cp in late_copies() + sends(True):
            cp.wait()

    @pl.when(core != 0)
    def _():
        for cp in sends(False):
            cp.start()
        for cp in sends(False):
            cp.wait()

    for cp in heads:
        cp.wait()


def project_kernel(x_ref, c_ref, w_in_ref, w_out_ref, ls_ref, proj, scales, sq_ref, xt_ref, ct_ref, wide):
    z = lax.axis_index(Z)
    xv = x_ref[...]
    ls = ls_ref[...]
    w2 = (w_out_ref[...].astype(F32) * ls).astype(BF)
    proj[:T] = mm(xv, w_in_ref[...]).astype(BF)
    proj[T : 2 * T] = mm(xv, w2, NT).astype(BF)
    proj[2 * T :] = mm(c_ref[...], w2, NT).astype(BF)
    top = ls.astype(BF).astype(F32)
    low_part = ls - top
    bands = [part[:, BAND * j : BAND * (j + 1)] for part in (top, low_part) for j in range(4)]
    bands = jnp.concatenate(bands, axis=0)
    for k in range(S):
        main = [bands[:, QUARTER * e + 16 * k : QUARTER * e + 16 * k + 16] for e in range(S)]
        rest = [bands[:, QUARTER * e + 128 + 2 * k : QUARTER * e + 130 + 2 * k] for e in range(S)]
        rest = jnp.concatenate(rest + [jnp.zeros((S, R - 16), F32)], axis=1)
        scales[k] = jnp.concatenate([jnp.concatenate(main, axis=1), rest], axis=0).astype(BF)
    xf = xv.astype(F32)
    sq_ref[...] = jnp.sum(xf * xf, axis=1, keepdims=True)
    mine = swap_units(16, z)
    for src, dst in ((x_ref, xt_ref), (c_ref, ct_ref)):
        for t in range(D // R):
            wide[t * R : (t + 1) * R, :] = src[:, t * R : (t + 1) * R].astype(F32).T.astype(BF)
        for j in range(4):
            left = []
            for e in range(S):
                at = BAND * j + QUARTER * e
                dst[R * j + 16 * e : R * j + 16 * e + 16] = wide[pl.ds(pl.multiple_of(at + 16 * z, 16), 16), :]
                left.append(wide[at + 128 : at + QUARTER])
            dst[512 + 16 * j : 512 + 16 * j + 16] = mm(mine, jnp.concatenate(left, axis=0)).astype(BF)


def gram_kernel(got_ref, w_in_ref, w_out_ref, ls_ref, proj_ref, scales_ref, out_ref):
    z = lax.axis_index(Z)
    for k in range(S):
        out_ref[k, 32 : 32 + 3 * T] = proj_ref[...]
        out_ref[k, 32 + 3 * T :] = scales_ref[k]
    ls = ls_ref[...]
    first, second = [], []
    for u in range(9):
        block = got_ref[:, 16 * u : 16 * u + 16, :].astype(F32)
        for part in (block[:, :8], block[:, 8:]):
            part = part.reshape(4, 2, 8, R)
            a, b = halves(part[:, 0], part[:, 1])
            first.append(a.reshape(32, R).astype(BF))
            second.append(b.reshape(32, R).astype(BF))
    first = jnp.concatenate(first, axis=1)
    second = jnp.concatenate(second, axis=1)
    up = mm(first, w_in_ref[:HALF]) + mm(second, w_in_ref[HALF:])
    down = mm((first.astype(F32) * ls[:, :HALF]).astype(BF), w_out_ref[:, :HALF], NT)
    down = down + mm((second.astype(F32) * ls[:, HALF:]).astype(BF), w_out_ref[:, HALF:], NT)
    below = (lax.broadcasted_iota(jnp.int32, (32, R), 0) // 4) < z
    out = jnp.where(below, up, down).astype(BF)
    for k in range(S):
        out_ref[k, :32] = out


def spread_kernel(part_ref, out_ref, sem):
    copies = [pltpu.make_async_copy(part_ref.at[:, pl.ds(0, 32)], out_ref.at[i], sem.at[i]) for i in range(16)]
    for cp in copies:
        cp.start()
    for cp in copies:
        cp.wait()


def main_kernel(own_ref, oth_ref, *refs):
    proj_ref, sq_ref, wown_ref, woth_ref, xt_ref, ct_ref, gown_ref, goth_ref, norm_ref = refs[:9]
    kmat, pre, qacc, hacc, slope, hs, hts, sts, wbuf, xs, gos, lefts, sem = refs[9:]
    core = lax.axis_index(C)
    is0 = core == 0
    copies = []
    for i in range(4):
        slot = (lax.axis_index(X) + 4 - i) % 4
        for n, (ref, half) in enumerate(((wown_ref, core), (woth_ref, 1 - core))):
            copies.append(pltpu.make_async_copy(ref.at[i], wbuf.at[half, slot], sem.at[i * 2 + n]))
    for cp in copies:
        cp.start()

    def place(s, carry):
        cols = pl.ds(pl.multiple_of(s * R, R), R)
        for x in range(4):
            own = [own_ref[y * 4 + x, s].astype(F32).reshape(4, 8, R) for y in range(4)]
            oth = [oth_ref[y * 4 + x, s].astype(F32).reshape(4, 8, R) for y in range(4)]
            for c in range(2):
                v = [jnp.where(is0, a, b) if c == 0 else jnp.where(is0, b, a) for a, b in zip(own, oth)]
                e01, o01 = halves(v[0], v[1])
                e23, o23 = halves(v[2], v[3])
                ev = jnp.concatenate([e01, e23], axis=1).astype(BF)
                od = jnp.concatenate([o01, o23], axis=1).astype(BF)
                for i in range(4):
                    row = (x * 2 + c) * 16
                    kmat[2 * i * R + row : 2 * i * R + row + 16, cols] = ev[i]
                    kmat[(2 * i + 1) * R + row : (2 * i + 1) * R + row + 16, cols] = od[i]
        return carry

    lax.fori_loop(0, S, place, 0)
    for s in range(S):
        for i, acc in enumerate((pre, qacc, hacc)):
            acc[:, s * R : (s + 1) * R] = proj_ref[s, 32 + T * i : 32 + T * (i + 1)].astype(F32)
    sq = sq_ref[...]
    for cp in copies:
        cp.wait()

    def weights(kind, s):
        return jnp.concatenate([wbuf[kind, j, s, :128] for j in range(4)] + [wbuf[kind, j, s, 128:] for j in range(4)], axis=0)

    lane = lax.broadcasted_iota(jnp.int32, (T, R), 1)
    scal = jnp.zeros((T, R), F32)
    inv = []
    x = xt_ref[...]
    xs[0] = x
    for s in range(S):
        here = slice(s * R, (s + 1) * R)
        r = lax.rsqrt(sq * (1.0 / D) + EPS)
        inv.append(r)
        scal = jnp.where(lane == s, r, scal)
        v = pre[:, here] * r
        pre[:, here] = v
        th = jnp.tanh(GELU_A * (v + GELU_B * v * v * v))
        h = (0.5 * v * (1.0 + th)).astype(BF)
        slope[:, here] = 0.5 * (1.0 + th) + 0.5 * v * (1.0 - th * th) * (GELU_A * (1.0 + 3.0 * GELU_B * v * v))
        hs[s] = h
        hf = h.astype(F32)
        if s + 1 < S:
            before = qacc[:, here]
            qacc[:, s * R :] += mm(h, kmat[s * R :, here], NT)
            sq = jnp.maximum(sq + jnp.sum(hf * (before + qacc[:, here]), axis=1, keepdims=True), 0.0)
            pre[:, (s + 1) * R :] += mm(h, kmat[here, (s + 1) * R :])
            x = (x.astype(F32) + mm(weights(1, s), h, NT)).astype(BF)
            xs[s + 1] = x
        hts[s] = hf.T.astype(BF)
    sts[...] = scal.T
    gam = jnp.zeros((T, 1), F32)
    total = jnp.zeros((64, R), F32)
    g = ct_ref[...]
    for s in reversed(range(S)):
        here = slice(s * R, (s + 1) * R)
        hg = hacc[:, here]
        if s + 1 < S:
            hg = hg - gam * qacc[:, here]
        p = (hg * slope[:, here]).astype(BF)
        r = inv[s]
        cen = r * r * (jnp.sum(p.astype(F32) * pre[:, here], axis=1, keepdims=True) * (1.0 / D))
        if s > 0:
            upd = r * mm(p, kmat[: s * R, here], NT)
            if s + 1 < S:
                upd = upd - gam * mm(hs[s], kmat[here, : s * R])
            hacc[:, : s * R] += upd
        gam = gam + cen

        xf = xs[s].astype(F32)
        rrow = sts[s : s + 1, :]
        gi = mm((xf * rrow).astype(BF), p)
        for j in range(9):
            total = total + gi[64 * j : 64 * j + 64] * gi[64 * j : 64 * j + 64]
        for i in range(16):
            a, b = gi[32 * i : 32 * i + 16], gi[32 * i + 16 : 32 * i + 32]
            gown_ref[i, 16 * s : 16 * s + 16] = jnp.where(is0, a, b).astype(BF)
            goth_ref[i, 16 * s : 16 * s + 16] = jnp.where(is0, b, a).astype(BF)
        for j in range(4):
            lefts[j, 16 * s : 16 * s + 16] = gi[512 + 16 * j : 512 + 16 * j + 16].astype(BF)
        lsf = proj_ref[s, 32 + 3 * T :].astype(F32)
        lsf = jnp.concatenate([lsf[:4] + lsf[4:8], lsf[8:12] + lsf[12:]], axis=0)
        lrow = jnp.concatenate([lsf[j : j + 1] for j in range(4)] + [lsf[4 + j : 5 + j, :16] for j in range(4)], axis=1)
        gos[s] = mm(hts[s], g, NT) * lrow
        if s > 0:
            crow = jnp.broadcast_to(cen, (T, R)).T[:1]
            g = (g.astype(F32) + rrow * mm(weights(0, s), p, NT) - crow * xf).astype(BF)
    units = swap_units(R)
    for j in range(4):
        left = mm(units, lefts[j])
        for i in range(4):
            a, b = left[32 * i : 32 * i + 16], left[32 * i + 16 : 32 * i + 32]
            gown_ref[4 * j + i, 128:ROWS] = jnp.where(is0, a, b).astype(BF)
            goth_ref[4 * j + i, 128:ROWS] = jnp.where(is0, b, a).astype(BF)
    acc = jnp.zeros((R, SLICE), F32)
    for s in range(S):
        acc = acc + gos[s] * gos[s]
    tails = []
    for quad in range(2):
        v = [gos[quad * 4 + i].reshape(16, 8, SLICE) for i in range(4)]
        a0, a1 = halves(v[0], v[1])
        b0, b1 = halves(v[2], v[3])
        even = jnp.concatenate([a0, b0], axis=1)
        odd = jnp.concatenate([a1, b1], axis=1)
        mine = jnp.where(is0, even, odd)
        rest = jnp.where(is0, odd, even)
        for t in range(4):
            at = slice(ROWS + 32 * t + 16 * quad, ROWS + 32 * t + 16 * quad + 16)
            gown_ref[:, at] = mine[:, :, t * R : (t + 1) * R].astype(BF)
            goth_ref[:, at] = rest[:, :, t * R : (t + 1) * R].astype(BF)
        tails.append((mine[:, :, 4 * R :], rest[:, :, 4 * R :]))
    gown_ref[:, ROWS + 128 :] = jnp.concatenate([tails[0][0], tails[1][0]], axis=2).astype(BF)
    goth_ref[:, ROWS + 128 :] = jnp.concatenate([tails[0][1], tails[1][1]], axis=2).astype(BF)
    one = jnp.sum(jnp.sum(total, axis=0, keepdims=True), axis=1, keepdims=True)
    two = jnp.sum(jnp.sum(acc, axis=0, keepdims=True), axis=1, keepdims=True)
    norm_ref[...] = jnp.broadcast_to((one + two).reshape(1, 1, 1), (2 * S, 8, R))


def mix_kernel(norm_ref, own_ref, got_ref, out_ref):
    core = lax.axis_index(C)
    sums = [norm_ref[0][:1], norm_ref[1][:1]]
    for k in range(1, S):
        for c in range(2):
            sums[c] = sums[c] + norm_ref[2 * k + c][:1]
    even, odd = (CLIP_NORM / (jnp.sqrt(v) + CLIP_OFFSET) for v in sums)
    mine = jnp.where(core == 0, even, odd)
    other = jnp.where(core == 0, odd, even)
    for i in range(16):
        out_ref[i] = (own_ref[i].astype(F32) * mine + got_ref[i].astype(F32) * other).astype(BF)


def sum_kernel(got_ref, out_ref):
    total = got_ref[0].astype(F32)
    for i in range(1, 16):
        total = total + got_ref[i].astype(F32)
    tiles = [total[ROWS + 32 * t : ROWS + 32 * t + 32].reshape(4, 8, R) for t in range(4)]
    last = total[ROWS + 128 :]
    tail = jnp.concatenate([last[:, :64], last[:, 64:]], axis=0)
    tail = jnp.concatenate([tail, jnp.zeros((32, 64), F32)], axis=1).reshape(4, 8, R)
    first = halves(tiles[0], tiles[1])
    second = halves(tiles[2], tiles[3])
    third = (tail, pltpu.roll(tail, 4, axis=1))
    for s in range(S):
        left = total[128 + 8 * (s // 4) : 136 + 8 * (s // 4)]
        if s % 4:
            left = pltpu.roll(left, 8 - 2 * (s % 4), axis=0)
        parts = [total[16 * s : 16 * s + 16]] + [v[s % 2][s // 2] for v in (first, second, third)] + [left]
        out_ref[s] = jnp.concatenate(parts, axis=0).astype(BF)


def join_kernel(got_ref, out_ref, in_ref):
    row = lax.broadcasted_iota(jnp.int32, (8, R), 0)
    mains, rests, left = [], [], [None, None]
    for k in range(S):
        got = got_ref[k].astype(F32)
        in_ref[0, 16 * k : 16 * k + 16] = got[:16]
        unit = got[40:]
        if k % 4:
            unit = pltpu.roll(unit, 2 * (k % 4), axis=0)
        left[k // 4] = unit if k % 4 == 0 else jnp.where(row // 2 == k % 4, unit, left[k // 4])
        mains.append(got[16:32])
        tail = jnp.concatenate([got[32:36, 16 * j : 16 * j + 16] for j in range(4)], axis=0)
        rests.append(tail)
    in_ref[0, 128:136] = left[0]
    in_ref[0, 136:] = left[1]
    pieces = []
    for e in range(S):
        pieces += [v[:, 16 * e : 16 * e + 16] for v in mains]
        pieces += [v[:, 2 * e : 2 * e + 2] for v in rests]
    whole = jnp.concatenate(pieces, axis=1)
    for j in range(4):
        out_ref[0, :, BAND * j : BAND * (j + 1)] = whole[4 * j : 4 * j + 4]


def shifted(value, axis, size):
    return [lax.ppermute(value, axis, [(i, (i + d) % size) for i in range(size)]) for d in range(1, size)]


def per_device(inputs, w_in, w_out, layer_scale, cotangent):
    swap = [(0, 1), (1, 0)]
    w1 = w_in[0]
    flops = 2 * T * D * R
    anywhere = pl.BlockSpec(memory_space=pl.ANY)

    far = pl.BlockSpec(memory_space=pltpu.HBM)
    (pay,) = call(
        pack_kernel, "pack",
        [((S, 2 * ROWS, R), BF)],
        [anywhere, anywhere, anywhere],
        [
            pltpu.VMEM((16, D), BF),
            pltpu.VMEM((R, BAND), BF),
            pltpu.VMEM((BAND, R), BF),
            pltpu.VMEM((S, ROWS, R), BF),
            pltpu.VMEM((ROWS, R), BF),
            pltpu.VMEM((1, D), F32),
            pltpu.SemaphoreType.DMA((LAST + 1,)),
        ],
        flops=flops // 16, size=2 << 20, vmem=PACK_VMEM, to=[far],
    )(w1, w_out[0], layer_scale)
    got = lax.all_to_all(pay, Z, 0, 0)

    proj, scales, sq, xt, ct = call(
        project_kernel, "project",
        [((3 * T, R), BF), ((S, 16, R), BF), ((T, 1), F32), ((SLICE, T), BF), ((SLICE, T), BF)],
        [VM, VM, VM, VM, VM],
        [pltpu.VMEM((D, T), BF)], flops=3 * flops, size=5 << 20, vmem=16,
    )(inputs, cotangent, w1, w_out[0], layer_scale)

    (part,) = call(
        gram_kernel, "gram", [((S, 48 + 3 * T, R), BF)], [VM] * 6,
        flops=flops // 2, size=3 << 20, vmem=12,
    )(got, w1, w_out[0], layer_scale, proj, scales)
    part, got = lax.optimization_barrier((part, got))
    part = lax.all_to_all(part, Z, 0, 0)
    own_w = got[:, ROWS : 2 * ROWS]
    own_w = jnp.stack([own_w] + shifted(own_w, X, 4))
    part, own_w = lax.optimization_barrier((part, own_w))

    (spread,) = call(
        spread_kernel, "spread", [((16, S, 32, R), BF)], [VM], [pltpu.SemaphoreType.DMA((16,))], to=[SPREAD]
    )(part)
    kown = lax.all_to_all(spread, (Y, X), 0, 0)
    kown, own_w = lax.optimization_barrier((kown, own_w))
    koth = lax.ppermute(kown, C, swap)
    other_w = lax.ppermute(own_w, C, swap)

    gown, goth, norm = call(
        main_kernel, "main",
        [((16, 2 * ROWS, R), BF), ((16, 2 * ROWS, R), BF), ((2 * S, 8, R), F32)],
        [VM, VM, VM, VM, anywhere, anywhere, VM, VM],
        [
            pltpu.VMEM((S * R, S * R), BF),
            pltpu.VMEM((T, S * R), F32),
            pltpu.VMEM((T, S * R), F32),
            pltpu.VMEM((T, S * R), F32),
            pltpu.VMEM((T, S * R), F32),
            pltpu.VMEM((S, T, R), BF),
            pltpu.VMEM((S, R, T), BF),
            pltpu.VMEM((R, T), F32),
            pltpu.VMEM((2, 4, S, QUARTER, R), BF),
            pltpu.VMEM((S, SLICE, T), BF),
            pltpu.VMEM((S, R, SLICE), F32),
            pltpu.VMEM((4, R, R), BF),
            pltpu.SemaphoreType.DMA((8,)),
        ],
        flops=2 * 32 * SLICE * T * R + 2 * 192 * T * R * R, size=10 << 20, trans=S * T * R, vmem=28,
    )(kown, koth, part, sq, own_w, other_w, xt, ct)

    ggot = lax.ppermute(goth, C, swap)
    norm = lax.all_to_all(norm, (Z, C), 0, 0)
    (both,) = call(mix_kernel, "mix", [((16, 2 * ROWS, R), BF)], [VM, VM, VM], size=4 << 20)(norm, gown, ggot)
    both = lax.all_to_all(both, (Y, X), 0, 0)
    (sent,) = call(sum_kernel, "sum", [((S, 48, R), BF)], [VM], size=2 << 20)(both)
    got = lax.all_to_all(sent, Z, 0, 0)
    grad_out, grad_in = call(join_kernel, "join", [((1, 4, D), F32), ((1, ROWS, R), F32)], [VM])(got)
    return grad_in, grad_out


def solution(mesh):
    split = Mesh(np.asarray(mesh.devices).reshape(S, 4, 4, 2), (Z, Y, X, C))
    dp = (Y, X, C)
    return jax.shard_map(
        per_device,
        mesh=split,
        in_specs=(P(dp, None), P(Z, None, None), P(Z, None, None), P(Z, None), P(dp, None)),
        out_specs=(P(Z, dp, None), P(Z, dp, None)),
        check_vma=False,
    )
```

```python
import jax
import jax.numpy as jnp
import numpy as np
from jax import lax
from jax.experimental import pallas as pl
from jax.experimental.pallas import tpu as pltpu
from jax.sharding import Mesh, PartitionSpec as P

EPS = 1e-06
CLIP_NORM = 256.0
CLIP_OFFSET = 0.01
S = 8
R = 128
T = 128
D = 4608
SLICE = D // S
QUARTER = SLICE // 4
PACK_VMEM = 56
LATE = 6
BAND = D // 4
THIRD = BAND // 3
LAST = 2 + 2 * S + S * S
Z, Y, X, C = "section", "y", "x", "core"
BF = jnp.bfloat16
F32 = jnp.float32
NN = (((1,), (0,)), ((), ()))
NT = (((1,), (1,)), ((), ()))
GELU_A = 0.7978845608028654
GELU_B = 0.044715
HALF = D // 2
ROWS = D * 4 // R
VM = pl.BlockSpec(memory_space=pltpu.VMEM)
SPREAD = VM


def mm(a, b, dims=NN):
    return lax.dot_general(a, b, dims, preferred_element_type=F32)


def halves(even, odd):
    low = lax.broadcasted_iota(jnp.int32, even.shape, 1) < 4
    return (
        jnp.where(low, even, pltpu.roll(odd, 4, axis=1)),
        jnp.where(low, pltpu.roll(even, 4, axis=1), odd),
    )


def call(kernel, name, outs, ins, scratch=(), flops=0, size=1 << 21, trans=0, vmem=8, to=None, alias=None):
    return pl.pallas_call(
        kernel,
        out_shape=tuple(jax.ShapeDtypeStruct(*o) for o in outs),
        in_specs=list(ins),
        out_specs=tuple(to or [VM] * len(outs)),
        scratch_shapes=list(scratch),
        input_output_aliases=alias or {},
        compiler_params=pltpu.CompilerParams(vmem_limit_bytes=vmem << 20),
        cost_estimate=pl.CostEstimate(flops=flops, bytes_accessed=size, transcendentals=trans),
        name=name,
    )


def swap_units(count, picked=None):
    row = lax.broadcasted_iota(jnp.int32, (count, R), 0)
    col = lax.broadcasted_iota(jnp.int32, (count, R), 1)
    outer = row // 16 if picked is None else picked
    return (col == ((row % 16) // 2) * 16 + outer * 2 + row % 2).astype(BF)


def pack_kernel(w_in_ref, w_out_ref, far_ls_ref, pay_ref, rows, wide, block, strip, head, ls_ref, sem):
    y, x, core = lax.axis_index(Y), lax.axis_index(X), lax.axis_index(C)
    q = (x * 2 + core) * 4 + y
    row_copy = pltpu.make_async_copy(w_out_ref.at[pl.ds(pl.multiple_of((q // 4) * 16, 16), 16)], rows, sem.at[0])
    row_copy.start()
    ls_copy = pltpu.make_async_copy(far_ls_ref, ls_ref, sem.at[LAST])
    ls_copy.start()
    start = pl.multiple_of(x * BAND, R)

    def in_copy():
        return pltpu.make_async_copy(w_in_ref.at[pl.ds(start, BAND)], block, sem.at[1])

    def out_copies():
        return [
            pltpu.make_async_copy(
                w_out_ref.at[:, pl.ds(pl.multiple_of(start + THIRD * i, R), THIRD)], wide.at[i], sem.at[10 + i]
            )
            for i in range(3)
        ]

    def late_copies():
        return [
            pltpu.make_async_copy(
                w_in_ref.at[pl.ds(pl.multiple_of(start + QUARTER * e + 16 * k, 16), 16)],
                pay_ref.at[k, pl.ds(ROWS + 16 * e, 16)],
                sem.at[2 + S + k * S + e],
            )
            for k in range(LATE)
            for e in range(S)
        ]

    @pl.when(core == 0)
    def _():
        for cp in late_copies():
            cp.start()
        in_copy().start()

    @pl.when(core != 0)
    def _():
        for cp in out_copies():
            cp.start()

    ls_copy.wait()
    row_copy.wait()
    part = rows[...].astype(F32) * ls_ref[...]
    group = q % 4
    mine = jnp.where(group < 2, part[:8], part[8:])
    turn = pltpu.roll(mine, 4, axis=0)
    odd = group % 2 == 1
    low = lax.broadcasted_iota(jnp.int32, (8, HALF), 0) < 4
    mine = jnp.where(
        low,
        jnp.where(odd, turn[:, :HALF], mine[:, :HALF]),
        jnp.where(odd, mine[:, HALF:], turn[:, HALF:]),
    )
    for u in range(9):
        two = jnp.concatenate([mine[:, 256 * u : 256 * u + R], mine[:, 256 * u + R : 256 * (u + 1)]], axis=0).astype(BF)
        head[16 * u : 16 * u + 16] = two
    heads = [pltpu.make_async_copy(head, pay_ref.at[k, pl.ds(0, ROWS)], sem.at[2 + k]) for k in range(S)]
    for cp in heads:
        cp.start()

    @pl.when(core == 0)
    def _():
        in_copy().wait()

    @pl.when(core != 0)
    def _():
        parts = out_copies()
        scale = ls_ref[:, pl.ds(start, BAND)]
        for t in range(BAND // R):
            if t % 3 == 0:
                parts[t // 3].wait()
            tile = wide[t // 3, :, t % 3 * R : (t % 3 + 1) * R].astype(F32) * scale[:, t * R : (t + 1) * R]
            block[t * R : (t + 1) * R, :] = tile.T.astype(BF)

    for k in range(S):
        for e in range(S):
            strip[k, 16 * e : 16 * e + 16] = block[QUARTER * e + 16 * k : QUARTER * e + 16 * k + 16]
    left = jnp.concatenate([block[QUARTER * e + 128 : QUARTER * (e + 1)] for e in range(S)], axis=0)
    left = mm(swap_units(R), left).astype(BF)
    for k in range(S):
        strip[k, 128:] = left[16 * k : 16 * k + 16]

    def sends(late):
        return [
            pltpu.make_async_copy(strip.at[k, pl.ds(128, 16)], pay_ref.at[k, pl.ds(ROWS + 128, 16)], sem.at[2 + S + S * S + k])
            if late and k < LATE
            else pltpu.make_async_copy(strip.at[k], pay_ref.at[k, pl.ds(ROWS, ROWS)], sem.at[2 + S + S * S + k])
            for k in range(S)
        ]

    @pl.when(core == 0)
    def _():
        for cp in sends(True):
            cp.start()
        for cp in late_copies() + sends(True):
            cp.wait()

    @pl.when(core != 0)
    def _():
        for cp in sends(False):
            cp.start()
        for cp in sends(False):
            cp.wait()

    for cp in heads:
        cp.wait()


def project_kernel(x_ref, c_ref, w_in_ref, w_out_ref, ls_ref, proj, scales, sq_ref, xt_ref, ct_ref, wide):
    z = lax.axis_index(Z)
    xv = x_ref[...]
    ls = ls_ref[...]
    w2 = (w_out_ref[...].astype(F32) * ls).astype(BF)
    proj[:T] = mm(xv, w_in_ref[...]).astype(BF)
    proj[T : 2 * T] = mm(xv, w2, NT).astype(BF)
    proj[2 * T :] = mm(c_ref[...], w2, NT).astype(BF)
    top = ls.astype(BF).astype(F32)
    low_part = ls - top
    bands = [part[:, BAND * j : BAND * (j + 1)] for part in (top, low_part) for j in range(4)]
    bands = jnp.concatenate(bands, axis=0)
    for k in range(S):
        main = [bands[:, QUARTER * e + 16 * k : QUARTER * e + 16 * k + 16] for e in range(S)]
        rest = [bands[:, QUARTER * e + 128 + 2 * k : QUARTER * e + 130 + 2 * k] for e in range(S)]
        rest = jnp.concatenate(rest + [jnp.zeros((S, R - 16), F32)], axis=1)
        scales[k] = jnp.concatenate([jnp.concatenate(main, axis=1), rest], axis=0).astype(BF)
    xf = xv.astype(F32)
    sq_ref[...] = jnp.sum(xf * xf, axis=1, keepdims=True)
    mine = swap_units(16, z)
    for src, dst in ((x_ref, xt_ref), (c_ref, ct_ref)):
        for t in range(D // R):
            wide[t * R : (t + 1) * R, :] = src[:, t * R : (t + 1) * R].astype(F32).T.astype(BF)
        for j in range(4):
            left = []
            for e in range(S):
                at = BAND * j + QUARTER * e
                dst[R * j + 16 * e : R * j + 16 * e + 16] = wide[pl.ds(pl.multiple_of(at + 16 * z, 16), 16), :]
                left.append(wide[at + 128 : at + QUARTER])
            dst[512 + 16 * j : 512 + 16 * j + 16] = mm(mine, jnp.concatenate(left, axis=0)).astype(BF)


def gram_kernel(got_ref, w_in_ref, w_out_ref, ls_ref, proj_ref, scales_ref, out_ref):
    z = lax.axis_index(Z)
    for k in range(S):
        out_ref[k, 32 : 32 + 3 * T] = proj_ref[...]
        out_ref[k, 32 + 3 * T :] = scales_ref[k]
    ls = ls_ref[...]
    first, second = [], []
    for u in range(9):
        block = got_ref[:, 16 * u : 16 * u + 16, :].astype(F32)
        for part in (block[:, :8], block[:, 8:]):
            part = part.reshape(4, 2, 8, R)
            a, b = halves(part[:, 0], part[:, 1])
            first.append(a.reshape(32, R).astype(BF))
            second.append(b.reshape(32, R).astype(BF))
    first = jnp.concatenate(first, axis=1)
    second = jnp.concatenate(second, axis=1)
    up = mm(first, w_in_ref[:HALF]) + mm(second, w_in_ref[HALF:])
    down = mm((first.astype(F32) * ls[:, :HALF]).astype(BF), w_out_ref[:, :HALF], NT)
    down = down + mm((second.astype(F32) * ls[:, HALF:]).astype(BF), w_out_ref[:, HALF:], NT)
    below = (lax.broadcasted_iota(jnp.int32, (32, R), 0) // 4) < z
    out = jnp.where(below, up, down).astype(BF)
    for k in range(S):
        out_ref[k, :32] = out


def spread_kernel(part_ref, out_ref, sem):
    copies = [pltpu.make_async_copy(part_ref.at[:, pl.ds(0, 32)], out_ref.at[i], sem.at[i]) for i in range(16)]
    for cp in copies:
        cp.start()
    for cp in copies:
        cp.wait()


def main_kernel(own_ref, oth_ref, *refs):
    proj_ref, sq_ref, wown_ref, woth_ref, xt_ref, ct_ref, gown_ref, goth_ref, norm_ref = refs[:9]
    kmat, pre, qacc, hacc, slope, hs, hts, sts, wbuf, xs, gos, lefts, sem = refs[9:]
    core = lax.axis_index(C)
    is0 = core == 0
    copies = []
    for i in range(4):
        slot = (lax.axis_index(X) + 4 - i) % 4
        for n, (ref, half) in enumerate(((wown_ref, core), (woth_ref, 1 - core))):
            copies.append(pltpu.make_async_copy(ref.at[i], wbuf.at[half, slot], sem.at[i * 2 + n]))
    for cp in copies:
        cp.start()

    def place(s, carry):
        cols = pl.ds(pl.multiple_of(s * R, R), R)
        for x in range(4):
            own = [own_ref[y * 4 + x, s].astype(F32).reshape(4, 8, R) for y in range(4)]
            oth = [oth_ref[y * 4 + x, s].astype(F32).reshape(4, 8, R) for y in range(4)]
            for c in range(2):
                v = [jnp.where(is0, a, b) if c == 0 else jnp.where(is0, b, a) for a, b in zip(own, oth)]
                e01, o01 = halves(v[0], v[1])
                e23, o23 = halves(v[2], v[3])
                ev = jnp.concatenate([e01, e23], axis=1).astype(BF)
                od = jnp.concatenate([o01, o23], axis=1).astype(BF)
                for i in range(4):
                    row = (x * 2 + c) * 16
                    kmat[2 * i * R + row : 2 * i * R + row + 16, cols] = ev[i]
                    kmat[(2 * i + 1) * R + row : (2 * i + 1) * R + row + 16, cols] = od[i]
        return carry

    lax.fori_loop(0, S, place, 0)
    for s in range(S):
        for i, acc in enumerate((pre, qacc, hacc)):
            acc[:, s * R : (s + 1) * R] = proj_ref[s, 32 + T * i : 32 + T * (i + 1)].astype(F32)
    sq = sq_ref[...]
    for cp in copies:
        cp.wait()

    def weights(kind, s):
        return jnp.concatenate([wbuf[kind, j, s, :128] for j in range(4)] + [wbuf[kind, j, s, 128:] for j in range(4)], axis=0)

    lane = lax.broadcasted_iota(jnp.int32, (T, R), 1)
    scal = jnp.zeros((T, R), F32)
    inv = []
    x = xt_ref[...]
    xs[0] = x
    for s in range(S):
        here = slice(s * R, (s + 1) * R)
        r = lax.rsqrt(sq * (1.0 / D) + EPS)
        inv.append(r)
        scal = jnp.where(lane == s, r, scal)
        v = pre[:, here] * r
        pre[:, here] = v
        th = jnp.tanh(GELU_A * (v + GELU_B * v * v * v))
        h = (0.5 * v * (1.0 + th)).astype(BF)
        slope[:, here] = 0.5 * (1.0 + th) + 0.5 * v * (1.0 - th * th) * (GELU_A * (1.0 + 3.0 * GELU_B * v * v))
        hs[s] = h
        hf = h.astype(F32)
        if s + 1 < S:
            before = qacc[:, here]
            qacc[:, s * R :] += mm(h, kmat[s * R :, here], NT)
            sq = jnp.maximum(sq + jnp.sum(hf * (before + qacc[:, here]), axis=1, keepdims=True), 0.0)
            pre[:, (s + 1) * R :] += mm(h, kmat[here, (s + 1) * R :])
            x = (x.astype(F32) + mm(weights(1, s), h, NT)).astype(BF)
            xs[s + 1] = x
        hts[s] = hf.T.astype(BF)
    sts[...] = scal.T
    gam = jnp.zeros((T, 1), F32)
    total = jnp.zeros((64, R), F32)
    acc = jnp.zeros((R, SLICE), F32)
    tails = {}
    g = ct_ref[...]
    for s in reversed(range(S)):
        here = slice(s * R, (s + 1) * R)
        hg = hacc[:, here]
        if s + 1 < S:
            hg = hg - gam * qacc[:, here]
        p = (hg * slope[:, here]).astype(BF)
        r = inv[s]
        cen = r * r * (jnp.sum(p.astype(F32) * pre[:, here], axis=1, keepdims=True) * (1.0 / D))
        if s > 0:
            upd = r * mm(p, kmat[: s * R, here], NT)
            if s + 1 < S:
                upd = upd - gam * mm(hs[s], kmat[here, : s * R])
            hacc[:, : s * R] += upd
        gam = gam + cen

        xf = xs[s].astype(F32)
        rrow = sts[s : s + 1, :]
        gi = mm((xf * rrow).astype(BF), p)
        for j in range(9):
            total = total + gi[64 * j : 64 * j + 64] * gi[64 * j : 64 * j + 64]
        for i in range(16):
            a, b = gi[32 * i : 32 * i + 16], gi[32 * i + 16 : 32 * i + 32]
            gown_ref[i, 16 * s : 16 * s + 16] = jnp.where(is0, a, b).astype(BF)
            goth_ref[i, 16 * s : 16 * s + 16] = jnp.where(is0, b, a).astype(BF)
        for j in range(4):
            lefts[j, 16 * s : 16 * s + 16] = gi[512 + 16 * j : 512 + 16 * j + 16].astype(BF)
        lsf = proj_ref[s, 32 + 3 * T :].astype(F32)
        lsf = jnp.concatenate([lsf[:4] + lsf[4:8], lsf[8:12] + lsf[12:]], axis=0)
        lrow = jnp.concatenate([lsf[j : j + 1] for j in range(4)] + [lsf[4 + j : 5 + j, :16] for j in range(4)], axis=1)
        part = mm(hts[s], g, NT) * lrow
        acc = acc + part * part
        gos[s] = part
        if s > 0:
            crow = jnp.broadcast_to(cen, (T, R)).T[:1]
            g = (g.astype(F32) + rrow * mm(weights(0, s), p, NT) - crow * xf).astype(BF)
        if s % 4 == 0:
            v = [gos[s + i].reshape(16, 8, SLICE) for i in range(4)]
            a0, a1 = halves(v[0], v[1])
            b0, b1 = halves(v[2], v[3])
            even = jnp.concatenate([a0, b0], axis=1)
            odd = jnp.concatenate([a1, b1], axis=1)
            mine = jnp.where(is0, even, odd)
            rest = jnp.where(is0, odd, even)
            for t in range(4):
                at = slice(ROWS + 32 * t + 4 * s, ROWS + 32 * t + 4 * s + 16)
                gown_ref[:, at] = mine[:, :, t * R : (t + 1) * R].astype(BF)
                goth_ref[:, at] = rest[:, :, t * R : (t + 1) * R].astype(BF)
            tails[s // 4] = (mine[:, :, 4 * R :], rest[:, :, 4 * R :])
    units = swap_units(R)
    for j in range(4):
        left = mm(units, lefts[j])
        for i in range(4):
            a, b = left[32 * i : 32 * i + 16], left[32 * i + 16 : 32 * i + 32]
            gown_ref[4 * j + i, 128:ROWS] = jnp.where(is0, a, b).astype(BF)
            goth_ref[4 * j + i, 128:ROWS] = jnp.where(is0, b, a).astype(BF)
    gown_ref[:, ROWS + 128 :] = jnp.concatenate([tails[0][0], tails[1][0]], axis=2).astype(BF)
    goth_ref[:, ROWS + 128 :] = jnp.concatenate([tails[0][1], tails[1][1]], axis=2).astype(BF)
    one = jnp.sum(jnp.sum(total, axis=0, keepdims=True), axis=1, keepdims=True)
    two = jnp.sum(jnp.sum(acc, axis=0, keepdims=True), axis=1, keepdims=True)
    norm_ref[...] = jnp.broadcast_to((one + two).reshape(1, 1, 1), (2 * S, 8, R))


def mix_kernel(norm_ref, own_ref, got_ref, out_ref):
    core = lax.axis_index(C)
    sums = [norm_ref[0][:1], norm_ref[1][:1]]
    for k in range(1, S):
        for c in range(2):
            sums[c] = sums[c] + norm_ref[2 * k + c][:1]
    even, odd = (CLIP_NORM / (jnp.sqrt(v) + CLIP_OFFSET) for v in sums)
    mine = jnp.where(core == 0, even, odd)
    other = jnp.where(core == 0, odd, even)
    for i in range(16):
        out_ref[i] = (own_ref[i].astype(F32) * mine + got_ref[i].astype(F32) * other).astype(BF)


def sum_kernel(got_ref, out_ref):
    total = got_ref[0].astype(F32)
    for i in range(1, 16):
        total = total + got_ref[i].astype(F32)
    tiles = [total[ROWS + 32 * t : ROWS + 32 * t + 32].reshape(4, 8, R) for t in range(4)]
    last = total[ROWS + 128 :]
    tail = jnp.concatenate([last[:, :64], last[:, 64:]], axis=0)
    tail = jnp.concatenate([tail, jnp.zeros((32, 64), F32)], axis=1).reshape(4, 8, R)
    first = halves(tiles[0], tiles[1])
    second = halves(tiles[2], tiles[3])
    third = (tail, pltpu.roll(tail, 4, axis=1))
    for s in range(S):
        left = total[128 + 8 * (s // 4) : 136 + 8 * (s // 4)]
        if s % 4:
            left = pltpu.roll(left, 8 - 2 * (s % 4), axis=0)
        parts = [total[16 * s : 16 * s + 16]] + [v[s % 2][s // 2] for v in (first, second, third)] + [left]
        out_ref[s] = jnp.concatenate(parts, axis=0).astype(BF)


def join_kernel(got_ref, out_ref, in_ref):
    row = lax.broadcasted_iota(jnp.int32, (8, R), 0)
    mains, rests, left = [], [], [None, None]
    for k in range(S):
        got = got_ref[k].astype(F32)
        in_ref[0, 16 * k : 16 * k + 16] = got[:16]
        unit = got[40:]
        if k % 4:
            unit = pltpu.roll(unit, 2 * (k % 4), axis=0)
        left[k // 4] = unit if k % 4 == 0 else jnp.where(row // 2 == k % 4, unit, left[k // 4])
        mains.append(got[16:32])
        tail = jnp.concatenate([got[32:36, 16 * j : 16 * j + 16] for j in range(4)], axis=0)
        rests.append(tail)
    in_ref[0, 128:136] = left[0]
    in_ref[0, 136:] = left[1]
    pieces = []
    for e in range(S):
        pieces += [v[:, 16 * e : 16 * e + 16] for v in mains]
        pieces += [v[:, 2 * e : 2 * e + 2] for v in rests]
    whole = jnp.concatenate(pieces, axis=1)
    for j in range(4):
        out_ref[0, :, BAND * j : BAND * (j + 1)] = whole[4 * j : 4 * j + 4]


def shifted(value, axis, size):
    return [lax.ppermute(value, axis, [(i, (i + d) % size) for i in range(size)]) for d in range(1, size)]


def per_device(inputs, w_in, w_out, layer_scale, cotangent):
    swap = [(0, 1), (1, 0)]
    w1 = w_in[0]
    flops = 2 * T * D * R
    anywhere = pl.BlockSpec(memory_space=pl.ANY)

    far = pl.BlockSpec(memory_space=pltpu.HBM)
    (pay,) = call(
        pack_kernel, "pack",
        [((S, 2 * ROWS, R), BF)],
        [anywhere, anywhere, anywhere],
        [
            pltpu.VMEM((16, D), BF),
            pltpu.VMEM((3, R, THIRD), BF),
            pltpu.VMEM((BAND, R), BF),
            pltpu.VMEM((S, ROWS, R), BF),
            pltpu.VMEM((ROWS, R), BF),
            pltpu.VMEM((1, D), F32),
            pltpu.SemaphoreType.DMA((LAST + 1,)),
        ],
        flops=flops // 16, size=2 << 20, vmem=PACK_VMEM, to=[far],
    )(w1, w_out[0], layer_scale)
    got = lax.all_to_all(pay, Z, 0, 0)

    proj, scales, sq, xt, ct = call(
        project_kernel, "project",
        [((3 * T, R), BF), ((S, 16, R), BF), ((T, 1), F32), ((SLICE, T), BF), ((SLICE, T), BF)],
        [VM, VM, VM, VM, VM],
        [pltpu.VMEM((D, T), BF)], flops=3 * flops, size=5 << 20, vmem=16,
    )(inputs, cotangent, w1, w_out[0], layer_scale)

    (part,) = call(
        gram_kernel, "gram", [((S, 48 + 3 * T, R), BF)], [VM] * 6,
        flops=flops // 2, size=3 << 20, vmem=12,
    )(got, w1, w_out[0], layer_scale, proj, scales)
    part, got = lax.optimization_barrier((part, got))
    part = lax.all_to_all(part, Z, 0, 0)
    own_w = got[:, ROWS : 2 * ROWS]
    own_w = jnp.stack([own_w] + shifted(own_w, X, 4))
    part, own_w = lax.optimization_barrier((part, own_w))

    (spread,) = call(
        spread_kernel, "spread", [((16, S, 32, R), BF)], [VM], [pltpu.SemaphoreType.DMA((16,))], to=[SPREAD]
    )(part)
    kown = lax.all_to_all(spread, (Y, X), 0, 0)
    kown, own_w = lax.optimization_barrier((kown, own_w))
    koth = lax.ppermute(kown, C, swap)
    other_w = lax.ppermute(own_w, C, swap)

    gown, goth, norm = call(
        main_kernel, "main",
        [((16, 2 * ROWS, R), BF), ((16, 2 * ROWS, R), BF), ((2 * S, 8, R), F32)],
        [VM, VM, VM, VM, anywhere, anywhere, VM, VM],
        [
            pltpu.VMEM((S * R, S * R), BF),
            pltpu.VMEM((T, S * R), F32),
            pltpu.VMEM((T, S * R), F32),
            pltpu.VMEM((T, S * R), F32),
            pltpu.VMEM((T, S * R), F32),
            pltpu.VMEM((S, T, R), BF),
            pltpu.VMEM((S, R, T), BF),
            pltpu.VMEM((R, T), F32),
            pltpu.VMEM((2, 4, S, QUARTER, R), BF),
            pltpu.VMEM((S, SLICE, T), BF),
            pltpu.VMEM((S, R, SLICE), F32),
            pltpu.VMEM((4, R, R), BF),
            pltpu.SemaphoreType.DMA((8,)),
        ],
        flops=2 * 32 * SLICE * T * R + 2 * 192 * T * R * R, size=10 << 20, trans=S * T * R, vmem=28,
    )(kown, koth, part, sq, own_w, other_w, xt, ct)

    ggot = lax.ppermute(goth, C, swap)
    norm = lax.all_to_all(norm, (Z, C), 0, 0)
    (both,) = call(mix_kernel, "mix", [((16, 2 * ROWS, R), BF)], [VM, VM, VM], size=4 << 20)(norm, gown, ggot)
    both = lax.all_to_all(both, (Y, X), 0, 0)
    (sent,) = call(sum_kernel, "sum", [((S, 48, R), BF)], [VM], size=2 << 20)(both)
    got = lax.all_to_all(sent, Z, 0, 0)
    grad_out, grad_in = call(join_kernel, "join", [((1, 4, D), F32), ((1, ROWS, R), F32)], [VM])(got)
    return grad_in, grad_out


def solution(mesh):
    split = Mesh(np.asarray(mesh.devices).reshape(S, 4, 4, 2), (Z, Y, X, C))
    dp = (Y, X, C)
    return jax.shard_map(
        per_device,
        mesh=split,
        in_specs=(P(dp, None), P(Z, None, None), P(Z, None, None), P(Z, None), P(dp, None)),
        out_specs=(P(Z, dp, None), P(Z, dp, None)),
        check_vma=False,
    )
```
